32 devices in a mesh: groups: 2 (over x), seq: 16 (over z, y, core).
Axes of the slice: x: 2, y: 2, z: 4, core: 2. Of those that a mesh axis runs over, the one named last changes fastest.
Arguments:
- inputs: bfloat16 [16384, 2560], P(('groups', 'seq')), parts along dimension 0, may hold values from -6 to 6
- raw_steps: float32 [16384, 40], P(('groups', 'seq')), parts along dimension 0, may hold values from -4 to 4
- input_map: bfloat16 [16384, 128], P(('groups', 'seq')), parts along dimension 0, may hold values from -0.875 to 0.875
- output_map: bfloat16 [16384, 128], P(('groups', 'seq')), parts along dimension 0, may hold values from -0.875 to 0.875
- decay_rates: float32 [40], replicated, may hold values from 6.1035156e-05 to 0.03
- skip_gain: float32 [40], replicated, may hold values from 0.5 to 1.5
- starts: int32 [16384], P(('groups', 'seq')), parts along dimension 0, may hold values from 0 to 1, as said below
- cotangent: bfloat16 [16384, 2560], P(('groups', 'seq')), parts along dimension 0, may hold values from -6 to 6
Outputs:
- outputs: bfloat16 [16384, 2560], P(('groups', 'seq')), parts along dimension 0
- grad_inputs: bfloat16 [16384, 2560], P(('groups', 'seq')), parts along dimension 0
- grad_steps: float32 [16384, 40], P(('groups', 'seq')), parts along dimension 0
- grad_input_map: bfloat16 [16384, 128], P(('groups', 'seq')), parts along dimension 0
- grad_output_map: bfloat16 [16384, 128], P(('groups', 'seq')), parts along dimension 0
The draws below stay inside these ranges and needn't reach their ends.
There are 2 independent parts, one for each index of `groups`. The reference program is written for one: setup_inputs(seed, part) draws one part's arguments, and reference() takes and returns one part's arrays. A program takes and returns all parts, laid end to end along the dimension named above; an argument that names none is the same for every part. Nothing has to cross between parts.
Inputs may be any that keep to these rules, and one draw needn't show every extreme that they name: `starts`: exactly 2 entries are 1, at positions drawn from the seed; all others are 0.
All inputs are finite; a program needn't handle non-finite values.
Results may differ from the reference program's by a relative error of at most 0.014.
Values sent between devices are 32-bit elements; how exact they have to be, the bound alone decides.
No kernel may reach another device: no remote copies, remote signals or barrier semaphores. Data moves between devices by JAX's collectives and lax.ppermute only.
A program may use at most 128 MiB of HBM per device.

```python
import math
import jax
import jax.numpy as jnp
from jax import lax

HEAD_DIM = 64
STATE = 128
HEADS = 40
SPAN = 256
TOKENS = 8192
RESETS = 2


def draw_starts(key, part):
    order = jax.random.permutation(key, TOKENS)
    chosen = order[:RESETS]
    return jnp.zeros((TOKENS,), jnp.int32).at[chosen].set(1)


def block_scale(key, extent, cuts, least, top_value):
    level, own = 1.0, jax.random.fold_in(key, 6)
    for dim, blocks in cuts:
        draws = jnp.exp(jax.random.uniform(jax.random.fold_in(own, dim), (blocks,), jnp.float32, least / len(cuts), top_value / len(cuts)))
        level = level * jnp.repeat(draws, extent[dim] // blocks).reshape([-1 if axis == dim else 1 for axis in range(len(extent))])
    return level


def bell_draw(stream_key, dims, scale, limit, split=(), kind=jnp.bfloat16):
    values = jax.random.normal(stream_key, dims, jnp.float32) * scale
    if len(split) > 0:
        values = block_scale(stream_key, dims, split, -0.22, 0.18) * values
    return jnp.clip(values, min=-limit, max=limit).astype(kind)


def setup_inputs(seed: int = 0, part: int = 0) -> dict:
    keys = jax.random.split(jax.random.key(seed), 9)
    part_keys = jax.random.split(jax.random.fold_in(keys[8], part), 9)
    return {
        "inputs": bell_draw(part_keys[0], (TOKENS, HEADS * HEAD_DIM), 1.0, 6.0, ((0, 16),)),
        "raw_steps": bell_draw(part_keys[1], (TOKENS, HEADS), 1.0, 4.0, ((0, 16),), jnp.float32),
        "input_map": bell_draw(part_keys[2], (TOKENS, STATE), (1.9 / (STATE * TOKENS) ** 0.25), 0.875, ((0, 16),)),
        "output_map": bell_draw(part_keys[3], (TOKENS, STATE), (1.9 / (STATE * TOKENS) ** 0.25), 0.875, ((0, 16),)),
        "decay_rates": jnp.clip(jnp.exp(jax.random.uniform(keys[4], (HEADS,), jnp.float32, math.log(6.103515625e-05), math.log(0.03))), 6.103515625e-05, 0.03),
        "skip_gain": jnp.clip(jax.random.uniform(keys[5], (HEADS,), jnp.float32, 0.5, 1.5), 0.5, 1.5),
        "starts": draw_starts(jax.random.fold_in(jax.random.fold_in(keys[8], part), 71), part),
        "cotangent": bell_draw(part_keys[7], (TOKENS, HEADS * HEAD_DIM), 1.0, 6.0, ((0, 16),)),
    }


def block_parts(in_block, raw_block, key_block, query_block, start_block, decay_rates, skip_gain):
    block_len = in_block.shape[0]
    head_count = decay_rates.shape[0]
    by_head = in_block.reshape(block_len, head_count, -1)
    step_size = jax.nn.softplus(raw_block)
    cumulative = jnp.cumsum(-step_size * decay_rates[None, :], axis=0)
    start_count = jnp.cumsum(start_block, axis=0, dtype=jnp.int32)
    position = jnp.arange(block_len, dtype=jnp.int32)
    allowed = (start_count[:, None] == start_count[None, :]) & (position[:, None] >= position[None, :])
    query_key = jnp.dot(query_block, key_block.T, preferred_element_type=jnp.float32)
    cum_heads = cumulative.T
    log_gap = jnp.where(allowed[None], cum_heads[:, :, None] - cum_heads[:, None, :], 0.0)
    weight = jnp.where(allowed[None], jnp.exp(log_gap) * query_key[None] * step_size.T[:, None, :], 0.0).astype(jnp.bfloat16)
    local_out = jnp.einsum('hts,shp->thp', weight, by_head, preferred_element_type=jnp.float32)
    local_out = local_out + skip_gain[None, :, None] * by_head.astype(jnp.float32)
    final_count = start_count[-1]
    tail_scale = jnp.where((start_count == final_count)[:, None], jnp.exp(cumulative[-1][None, :] - cumulative) * step_size, 0.0)
    scaled = (by_head * tail_scale[:, :, None]).astype(jnp.bfloat16)
    block_state = jnp.einsum('shp,sn->hpn', scaled, key_block, preferred_element_type=jnp.float32)
    block_decay = jnp.where(final_count == 0, jnp.exp(cumulative[-1]), 0.0)
    return (local_out.reshape(block_len, -1), block_state, block_decay)

def carried_part(carried, raw_block, query_block, start_block, decay_rates):
    step_size = jax.nn.softplus(raw_block)
    cumulative = jnp.cumsum(-step_size * decay_rates[None, :], axis=0)
    start_count = jnp.cumsum(start_block, axis=0, dtype=jnp.int32)
    lead_scale = jnp.where((start_count == 0)[:, None], jnp.exp(cumulative), 0.0)
    rounded_state = carried.astype(jnp.bfloat16)
    reached = jnp.einsum('tn,hpn->thp', query_block, rounded_state, preferred_element_type=jnp.float32)
    return (reached * lead_scale[:, :, None]).reshape(query_block.shape[0], -1)

def carried_grad(carried, raw_block, query_block, start_block, decay_rates, cot_block):
    reached, pullback = jax.vjp(lambda state_in: carried_part(state_in, raw_block, query_block, start_block, decay_rates), carried)
    return (reached, pullback(cot_block.astype(jnp.float32))[0])

def block_grads(in_block, raw_block, key_block, query_block, start_block, decay_rates, skip_gain, carried, cot_block, state_cot, decay_cot):

    def forward(in_value, raw_in, key_in, query_in):
        local_out, block_state, block_decay = block_parts(in_value, raw_in, key_in, query_in, start_block, decay_rates, skip_gain)
        return (local_out + carried_part(carried, raw_in, query_in, start_block, decay_rates), block_state, block_decay)
    _, pullback = jax.vjp(forward, in_block, raw_block, key_block, query_block)
    return pullback((cot_block.astype(jnp.float32), state_cot, decay_cot))

def reference(inputs, raw_steps, input_map, output_map, decay_rates, skip_gain, starts, cotangent):
    block_total = inputs.shape[0] // SPAN
    head_count = decay_rates.shape[0]
    head_size = inputs.shape[1] // head_count
    state_size = input_map.shape[1]

    def blocks(values):
        return values.reshape((block_total, SPAN) + values.shape[1:])
    in_blocks, raw_blocks, key_blocks, query_blocks, start_blocks, cot_blocks = [blocks(v) for v in (inputs, raw_steps, input_map, output_map, starts, cotangent)]
    local_outs, states, decays = lax.map(lambda packed: block_parts(packed[0], packed[1], packed[2], packed[3], packed[4], decay_rates, skip_gain), (in_blocks, raw_blocks, key_blocks, query_blocks, start_blocks))
    zero_state = jnp.zeros((head_count, head_size, state_size), jnp.float32)

    def forward_step(running, element):
        decay_now, block_state = element
        return (decay_now[:, None, None] * running + block_state, running)
    _, carried_all = lax.scan(forward_step, zero_state, (decays, states))

    def output_block(packed):
        local_out, carried, raw_block, query_block, start_block, cot_block = packed
        reached, direct = carried_grad(carried, raw_block, query_block, start_block, decay_rates, cot_block)
        return ((local_out + reached).astype(jnp.bfloat16), direct)
    produced, directs = lax.map(output_block, (local_outs, carried_all, raw_blocks, query_blocks, start_blocks, cot_blocks))

    def backward_step(following, element):
        decay_now, direct = element
        return (direct + decay_now[:, None, None] * following, following)
    _, state_grads = lax.scan(backward_step, zero_state, (decays, directs), reverse=True)
    decay_grads = lax.optimization_barrier(jnp.sum(state_grads * carried_all, axis=(2, 3)))

    def grad_block(packed):
        return block_grads(packed[0], packed[1], packed[2], packed[3], packed[4], decay_rates, skip_gain, packed[5], packed[6], packed[7], packed[8])
    grad_in, grad_raw, grad_key, grad_query = lax.map(grad_block, (in_blocks, raw_blocks, key_blocks, query_blocks, start_blocks, carried_all, cot_blocks, state_grads, decay_grads))
    return (produced.reshape(inputs.shape), grad_in.reshape(inputs.shape), grad_raw.reshape(raw_steps.shape), grad_key.reshape(input_map.shape), grad_query.reshape(output_map.shape))
```

```python
import functools

import jax
import jax.numpy as jnp
from jax import lax
from jax.experimental import pallas as pl
from jax.experimental.pallas import tpu as pltpu
from jax.sharding import PartitionSpec as P

CHUNKS = 2
TILE = 256
VMEM_BYTES = 48 * 1024 * 1024

F32 = jnp.float32
BF16 = jnp.bfloat16


def dot_nn(left, right):
    return lax.dot_general(left, right, (((1,), (0,)), ((), ())), preferred_element_type=F32)


def dot_nt(left, right):
    return lax.dot_general(left, right, (((1,), (1,)), ((), ())), preferred_element_type=F32)


def halves(value):
    high = value.astype(BF16)
    return high, (value - high.astype(F32)).astype(BF16)


def sum_dot(matrix, value):
    first = value.astype(BF16)
    rest = value - first.astype(F32)
    second = rest.astype(BF16)
    third = (rest - second.astype(F32)).astype(BF16)
    return dot_nn(matrix, first) + dot_nn(matrix, second) + dot_nn(matrix, third)


def head_spread(head_count, first_column, columns, head_size):
    row = lax.broadcasted_iota(jnp.int32, (2 * head_count, columns), 0)
    row = jnp.where(row >= head_count, row - head_count, row)
    column = lax.broadcasted_iota(jnp.int32, (2 * head_count, columns), 1) + first_column
    return jnp.where(row == column // head_size, 1.0, 0.0).astype(BF16)


def head_collect(head_count, first_column, columns, head_size):
    row = lax.broadcasted_iota(jnp.int32, (columns, head_count), 0) + first_column
    column = lax.broadcasted_iota(jnp.int32, (columns, head_count), 1)
    return jnp.where(row // head_size == column, 1.0, 0.0).astype(BF16)


def triangle(rows, lower):
    first = lax.broadcasted_iota(jnp.int32, (rows, rows), 0)
    second = lax.broadcasted_iota(jnp.int32, (rows, rows), 1)
    return (first >= second) if lower else (first <= second)


def start_counts(starts_row):
    rows = starts_row.shape[1]
    flags = starts_row.astype(F32)
    column = jnp.sum(jnp.where(triangle(rows, True), flags, 0.0), axis=1, keepdims=True)
    spread = jnp.broadcast_to(flags, (8, rows)).astype(BF16)
    row = dot_nn(spread, triangle(rows, False).astype(F32).astype(BF16))[:1]
    return column, row


def softplus(value):
    return jnp.maximum(value, 0.0) + jnp.log1p(jnp.exp(-jnp.abs(value)))


def prep_kernel(
    head_size, raw_ref, rate_ref, starts_ref, query_ref, key_ref,
    lead_ref, tail_ref, leadt_ref, tailt_ref, grow_ref, fall_ref, decay_ref, last_ref,
):
    rows, head_count = raw_ref.shape
    step = softplus(raw_ref[...])
    lower = triangle(rows, True).astype(F32).astype(BF16)
    cumulative = sum_dot(lower, -step * rate_ref[...])
    count, _ = start_counts(starts_ref[...])
    lead = jnp.where(count == 0.0, query_ref[...].astype(F32), 0.0)
    tail = jnp.where(count == count[rows - 1 :, :], key_ref[...].astype(F32), 0.0)
    lead_ref[...] = lead.astype(BF16)
    tail_ref[...] = tail.astype(BF16)
    leadt_ref[...] = lead.T.astype(BF16)
    tailt_ref[...] = tail.T.astype(BF16)
    fall_ref[...] = jnp.concatenate(halves(jnp.exp(cumulative)), axis=1)
    grow_ref[...] = jnp.concatenate(halves(jnp.exp(-cumulative) * step), axis=1)
    last = jnp.broadcast_to(jnp.exp(cumulative[rows - 1 :, :]), (8, head_count))
    channels = decay_ref.shape[1]
    spread = head_spread(head_count, 0, channels, head_size)
    last_wide = dot_nn(jnp.concatenate(halves(last), axis=1), spread)[:1]
    last_ref[...] = last_wide
    decay_ref[...] = jnp.where(count[rows - 1 :, :] == 0.0, last_wide, 0.0)


def states_kernel(
    head_count, head_size, first, place_ref, in_ref, cot_ref, grow_ref, fall_ref, leadt_ref,
    tailt_ref, last_ref, send_ref, keep_ref,
):
    columns = in_ref.shape[1]
    spread = head_spread(head_count, first + pl.program_id(0) * columns, columns, head_size)
    grown = (dot_nn(grow_ref[...], spread) * in_ref[...].astype(F32)).astype(BF16)
    fallen = (dot_nn(fall_ref[...], spread) * cot_ref[...].astype(F32)).astype(BF16)
    state = dot_nn(tailt_ref[...], grown) * last_ref[...]
    direct = dot_nn(leadt_ref[...], fallen)
    low, mid = place_ref[0] == 0, place_ref[1] == 0
    half = state.shape[0] // 2
    quarter = half // 2
    for chain, value in enumerate((state, direct)):
        sent = jnp.where(low, value[half:], value[:half])
        kept = jnp.where(low, value[:half], value[half:])
        for ref, part in ((send_ref, sent), (keep_ref, kept)):
            ref[chain, 0] = jnp.where(mid, part[quarter:], part[:quarter])
            ref[chain, 1] = jnp.where(mid, part[:quarter], part[quarter:])


def scores_kernel(
    head_count, head_size, steps, starts_ref, query_ref, key_ref, in_ref, cot_ref, grow_ref,
    fall_ref, score_ref, scoret_ref, dquery_ref, dkey_ref, total_ref,
):
    columns = in_ref.shape[1]
    rows = in_ref.shape[0]
    step = pl.program_id(0)
    spread = head_spread(head_count, step * columns, columns, head_size)
    grown = (dot_nn(grow_ref[...], spread) * in_ref[...].astype(F32)).astype(BF16)
    fallen = (dot_nn(fall_ref[...], spread) * cot_ref[...].astype(F32)).astype(BF16)
    product = dot_nt(fallen, grown)

    @pl.when(step == 0)
    def _():
        total_ref[...] = product

    @pl.when(step > 0)
    def _():
        total_ref[...] += product

    @pl.when(step == steps - 1)
    def _():
        column, row = start_counts(starts_ref[...])
        same = column == row
        allowed = same & triangle(rows, True)
        score_ref[...] = jnp.where(allowed, dot_nt(query_ref[...], key_ref[...]), 0.0).astype(BF16)
        scoret_ref[...] = jnp.where(
            same & triangle(rows, False), dot_nt(key_ref[...], query_ref[...]), 0.0
        ).astype(BF16)
        grads = jnp.where(allowed, total_ref[...], 0.0)
        dquery_ref[...] = dot_nn(grads.astype(BF16), key_ref[...])
        dkey_ref[...] = dot_nn(grads.T.astype(BF16), query_ref[...])


def arranged(low, mid, took_ref, own_ref, chain):
    parts = []
    for ref in (own_ref, took_ref):
        first = jnp.where(mid, ref[chain, 1], ref[chain, 0])
        second = jnp.where(mid, ref[chain, 0], ref[chain, 1])
        parts.append(jnp.concatenate([first, second], axis=0))
    own, took = parts
    return jnp.concatenate([jnp.where(low, own, took), jnp.where(low, took, own)], axis=0)


def finish_kernel(
    head_count, head_size, first, steps, place_ref, in_ref, cot_ref, took_ref, own_ref, skip_ref,
    decay_ref, last_ref, grow_ref, fall_ref, lead_ref, tail_ref, score_ref, scoret_ref, starts_ref,
    raw_ref, rate_ref, dquery_in, dkey_in,
    out_ref, din_ref, dquery_ref, dkey_ref, draw_ref,
    rise_ref, sink_ref, edge_ref, dlead_ref, dtail_ref,
):
    rows, columns = in_ref.shape
    step = pl.program_id(0)
    start_column = first + step * columns
    low, mid = place_ref[0] == 0, place_ref[1] == 0
    entering = arranged(low, mid, took_ref, own_ref, 0)
    leaving = arranged(low, mid, took_ref, own_ref, 1)
    spread = head_spread(head_count, start_column, columns, head_size)
    grow = dot_nn(grow_ref[...], spread)
    fall = dot_nn(fall_ref[...], spread)
    in_wide = in_ref[...].astype(F32)
    cot_wide = cot_ref[...].astype(F32)
    grown = (grow * in_wide).astype(BF16)
    fallen = (fall * cot_wide).astype(BF16)
    entering_bf = entering.astype(BF16)
    leaving_bf = (leaving * last_ref[...]).astype(BF16)

    produced = dot_nn(score_ref[...], grown) + dot_nn(lead_ref[...], entering_bf)
    out_ref[...] = (fall * produced + skip_ref[...] * in_wide).astype(BF16)
    behind = dot_nn(tail_ref[...], leaving_bf)
    pulled = dot_nn(scoret_ref[...], fallen) + behind
    din_ref[...] = (grow * pulled + skip_ref[...] * cot_wide).astype(BF16)

    collect = head_collect(head_count, start_column, columns, head_size)

    def by_head(value):
        high, rest = halves(value)
        return dot_nn(high, collect) + dot_nn(rest, collect)

    grown_wide = grown.astype(F32)
    rise = by_head(fallen.astype(F32) * produced)
    sink = by_head(grown_wide * pulled)
    edge_row = jnp.sum(grown_wide * behind, axis=0, keepdims=True) + decay_ref[...] * jnp.sum(
        entering * leaving, axis=0, keepdims=True
    )
    edge = by_head(jnp.broadcast_to(edge_row, (8, columns)))
    dlead = dot_nt(fallen, entering_bf)
    dtail = dot_nt(grown, leaving_bf)

    @pl.when(step == 0)
    def _():
        rise_ref[...] = rise
        sink_ref[...] = sink
        edge_ref[...] = edge
        dlead_ref[...] = dlead
        dtail_ref[...] = dtail

    @pl.when(step > 0)
    def _():
        rise_ref[...] += rise
        sink_ref[...] += sink
        edge_ref[...] += edge
        dlead_ref[...] += dlead
        dtail_ref[...] += dtail

    @pl.when(step == steps - 1)
    def _():
        count, _ = start_counts(starts_ref[...])
        dquery_ref[...] = dquery_in[...] + jnp.where(count == 0.0, dlead_ref[...], 0.0)
        dkey_ref[...] = dkey_in[...] + jnp.where(count == count[rows - 1 :, :], dtail_ref[...], 0.0)
        upper = triangle(rows, False).astype(F32).astype(BF16)
        later = sum_dot(upper, rise_ref[...] - sink_ref[...]) + edge_ref[:1]
        raw = raw_ref[...]
        dstep = sink_ref[...] / softplus(raw) - rate_ref[...] * later
        draw_ref[...] = dstep / (1.0 + jnp.exp(-raw))


def whole(shape):
    return pl.BlockSpec(shape, lambda i, *_: (0,) * len(shape))


def params():
    return pltpu.CompilerParams(vmem_limit_bytes=VMEM_BYTES)


def cost(flops, count):
    return pl.CostEstimate(flops=flops, bytes_accessed=count, transcendentals=0)


def local(inputs, raw_steps, input_map, output_map, decay_rates, skip_gain, starts, cotangent):
    rows, channels = inputs.shape
    head_count = decay_rates.shape[0]
    head_size = channels // head_count
    state_size = input_map.shape[1]
    width = channels // CHUNKS
    tiles = width // TILE
    quarter = state_size // 4

    index = lax.axis_index("seq")
    size = lax.axis_size("seq")
    planes = size // 4
    core, side, plane = index % 2, (index // 2) % 2, index // 4
    place = jnp.stack([core, side]).astype(jnp.int32)
    first_core = core == 0
    first_side = side == 0
    starts_row = starts.reshape(1, rows)
    rate_row = decay_rates.reshape(1, head_count)
    skip_row = jnp.repeat(skip_gain, head_size).reshape(1, channels)

    def shape(dims, kind=F32):
        return jax.ShapeDtypeStruct(dims, kind)

    lead, tail, leadt, tailt, grow, fall, decay, last = pl.pallas_call(
        functools.partial(prep_kernel, head_size),
        out_shape=(
            shape((rows, state_size), BF16),
            shape((rows, state_size), BF16),
            shape((state_size, rows), BF16),
            shape((state_size, rows), BF16),
            shape((rows, 2 * head_count), BF16),
            shape((rows, 2 * head_count), BF16),
            shape((1, channels)),
            shape((1, channels)),
        ),
        compiler_params=params(),
        name="prep",
    )(raw_steps, rate_row, starts_row, output_map, input_map)

    def pieces(chunk):
        first = chunk * tiles
        tile = pl.BlockSpec((rows, TILE), lambda i, *_: (0, first + i))
        row = pl.BlockSpec((1, TILE), lambda i, *_: (0, first + i))
        part = pl.BlockSpec((2, 2, quarter, TILE), lambda i, *_: (0, 0, 0, i))
        return tile, row, part

    def device_states(chunk):
        tile, row, part = pieces(chunk)
        half = shape((2, 2, quarter, width))
        return pl.pallas_call(
            functools.partial(states_kernel, head_count, head_size, chunk * width),
            out_shape=(half, half),
            grid_spec=pltpu.PrefetchScalarGridSpec(
                num_scalar_prefetch=1,
                grid=(tiles,),
                in_specs=[
                    tile, tile, whole(grow.shape), whole(fall.shape), whole(leadt.shape),
                    whole(tailt.shape), row,
                ],
                out_specs=(part, part),
            ),
            compiler_params=params(),
            cost_estimate=cost(
                4 * rows * state_size * width + 8 * rows * head_count * width, 6 * rows * width
            ),
            name="states",
        )(place, inputs, cotangent, grow, fall, leadt, tailt, last)

    def swap(value, bit):
        return lax.ppermute(value, "seq", [(i, i ^ bit) for i in range(size)])

    decay_other = swap(decay, 1)
    decay_first = jnp.where(first_core, decay, decay_other)
    decay_second = jnp.where(first_core, decay_other, decay)
    chip_decay = decay * decay_other
    chip_other = swap(chip_decay, 2)
    side_first = jnp.where(first_side, chip_decay, chip_other)
    side_second = jnp.where(first_side, chip_other, chip_decay)
    plane_decay = chip_decay * chip_other

    levels = planes.bit_length() - 1
    before, after, group = [None], [None], plane_decay
    for level in range(levels - 1):
        other = swap(group, 4 << level)
        upper = (plane >> level) % 2 == 1
        ones = jnp.ones_like(group)
        before_now = jnp.where(upper, other, ones)
        after_now = jnp.where(upper, ones, other)
        if level:
            before_now, after_now = before[-1] * before_now, after[-1] * after_now
        before.append(before_now)
        after.append(after_now)
        group = group * other

    def level_perms(level):
        span = 1 << level
        perms = []
        for shift in range(span):
            pairs = []
            for base in range(0, planes, 2 * span):
                pairs.append((base + span - 1, base + span + shift))
                pairs.append((base + span, base + span - 1 - shift))
            perms.append([(4 * a + r, 4 * b + r) for a, b in pairs for r in range(4)])
        return perms

    def chain(chunk, sent, kept):
        cols = slice(chunk * width, (chunk + 1) * width)
        came = swap(sent, 1)
        d_first, d_second = decay_first[:, cols], decay_second[:, cols]
        s_first = jnp.where(first_core, kept[0], came[0])
        s_second = jnp.where(first_core, came[0], kept[0])
        g_first = jnp.where(first_core, kept[1], came[1])
        g_second = jnp.where(first_core, came[1], kept[1])
        chip = jnp.stack([d_second * s_first + s_second, g_first + d_first * g_second])
        side_sent, side_kept = chip[:, 0], chip[:, 1]
        side_came = swap(side_sent, 2)
        e_first, e_second = side_first[:, cols], side_second[:, cols]
        t_first = jnp.where(first_side, side_kept[0], side_came[0])
        t_second = jnp.where(first_side, side_came[0], side_kept[0])
        h_first = jnp.where(first_side, side_kept[1], side_came[1])
        h_second = jnp.where(first_side, side_came[1], side_kept[1])
        plane_state = e_second * t_first + t_second
        plane_direct = h_first + e_first * h_second
        p_decay = plane_decay[:, cols]
        entering = leaving = None
        for level in range(levels):
            upper = (plane >> level) % 2 == 1
            if level:
                payload = jnp.where(
                    upper, p_decay * leaving + plane_direct, p_decay * entering + plane_state
                )
            else:
                payload = jnp.where(upper, plane_direct, plane_state)
            taken = None
            for perm in level_perms(level):
                moved = lax.ppermute(payload, "seq", perm)
                taken = moved if taken is None else taken + moved
            if level:
                entering = entering + jnp.where(upper, before[level][:, cols] * taken, 0.0)
                leaving = leaving + jnp.where(upper, 0.0, after[level][:, cols] * taken)
            else:
                entering = jnp.where(upper, taken, 0.0)
                leaving = jnp.where(upper, 0.0, taken)
        through = e_first * entering + t_first
        through_back = e_second * leaving + h_second
        mine = jnp.stack(
            [
                jnp.where(first_side, entering, through),
                jnp.where(first_side, through_back, leaving),
            ]
        )
        theirs = jnp.stack(
            [
                jnp.where(first_side, through, entering),
                jnp.where(first_side, leaving, through_back),
            ]
        )
        chip_in = jnp.stack([swap(theirs, 2), mine], axis=1)
        inner = d_first * chip_in[0] + s_first
        inner_back = d_second * chip_in[1] + g_second
        own = jnp.stack(
            [
                jnp.where(first_core, chip_in[0], inner),
                jnp.where(first_core, inner_back, chip_in[1]),
            ]
        )
        give = jnp.stack(
            [
                jnp.where(first_core, inner, chip_in[0]),
                jnp.where(first_core, chip_in[1], inner_back),
            ]
        )
        return swap(give, 1), own

    score_tiles = channels // TILE
    all_tile = pl.BlockSpec((rows, TILE), lambda i, *_: (0, i))

    def scores():
        square = (rows, rows)
        return pl.pallas_call(
            functools.partial(scores_kernel, head_count, head_size, score_tiles),
            out_shape=(
                shape(square, BF16), shape(square, BF16),
                shape((rows, state_size)), shape((rows, state_size)),
            ),
            grid_spec=pltpu.PrefetchScalarGridSpec(
                num_scalar_prefetch=0,
                grid=(score_tiles,),
                in_specs=[
                    whole(starts_row.shape), whole(output_map.shape), whole(input_map.shape),
                    all_tile, all_tile, whole(grow.shape), whole(fall.shape),
                ],
                out_specs=(
                    whole(square), whole(square),
                    whole((rows, state_size)), whole((rows, state_size)),
                ),
                scratch_shapes=[pltpu.VMEM(square, F32)],
            ),
            compiler_params=params(),
            cost_estimate=cost(2 * rows * rows * channels, 4 * rows * channels),
            name="scores",
        )(starts_row, output_map, input_map, inputs, cotangent, grow, fall)

    def finish(chunk, took, own, out, din, dquery, dkey):
        tile, row, part = pieces(chunk)
        square = (rows, rows)
        flat = (rows, state_size)
        per_head = (rows, head_count)
        operands = (
            place, inputs, cotangent, took, own, skip_row, decay, last, grow, fall, lead, tail,
            score, scoret, starts_row, raw_steps, rate_row, dquery, dkey,
        )
        return pl.pallas_call(
            functools.partial(finish_kernel, head_count, head_size, chunk * width, tiles),
            out_shape=(
                shape((rows, width), BF16), shape((rows, width), BF16),
                shape(flat), shape(flat), shape(per_head),
            ),
            grid_spec=pltpu.PrefetchScalarGridSpec(
                num_scalar_prefetch=1,
                grid=(tiles,),
                in_specs=[
                    tile, tile, part, part, row, row, row, whole(grow.shape), whole(fall.shape),
                    whole(flat), whole(flat), whole(square), whole(square),
                    whole(starts_row.shape), whole(per_head), whole(rate_row.shape),
                    whole(flat), whole(flat),
                ],
                out_specs=(
                    pl.BlockSpec((rows, TILE), lambda i, *_: (0, i)),
                    pl.BlockSpec((rows, TILE), lambda i, *_: (0, i)),
                    whole(flat), whole(flat), whole(per_head),
                ),
                scratch_shapes=[
                    pltpu.VMEM(per_head, F32), pltpu.VMEM(per_head, F32),
                    pltpu.VMEM((8, head_count), F32),
                    pltpu.VMEM(flat, F32), pltpu.VMEM(flat, F32),
                ],
            ),
            compiler_params=params(),
            cost_estimate=cost(4 * rows * rows * width, 12 * rows * width),
            name="finish",
        )(*operands)

    states = [device_states(chunk) for chunk in range(CHUNKS)]
    score, scoret, dquery, dkey = scores()
    outs, dins, draw = [], [], None
    for chunk in range(CHUNKS):
        took, own = chain(chunk, *states[chunk])
        out, din, dquery, dkey, draw_now = finish(chunk, took, own, None, None, dquery, dkey)
        outs.append(out)
        dins.append(din)
        draw = draw_now if draw is None else draw + draw_now
    return (
        jnp.concatenate(outs, axis=1),
        jnp.concatenate(dins, axis=1),
        draw,
        dkey.astype(BF16),
        dquery.astype(BF16),
    )


def solution(mesh):
    sequence = P(("groups", "seq"), None)
    return jax.shard_map(
        local,
        mesh=mesh,
        in_specs=(
            sequence, sequence, sequence, sequence, P(), P(), P(("groups", "seq")), sequence,
        ),
        out_specs=(sequence,) * 5,
        check_vma=False,
    )
```

```python
import functools

import jax
import jax.numpy as jnp
from jax import lax
from jax.experimental import pallas as pl
from jax.experimental.pallas import tpu as pltpu
from jax.sharding import PartitionSpec as P

CHUNKS = 2
TILE = 640
VMEM_BYTES = 24 * 1024 * 1024

F32 = jnp.float32
BF16 = jnp.bfloat16


def dot_nn(left, right):
    return lax.dot_general(left, right, (((1,), (0,)), ((), ())), preferred_element_type=F32)


def dot_nt(left, right):
    return lax.dot_general(left, right, (((1,), (1,)), ((), ())), preferred_element_type=F32)


def halves(value):
    high = value.astype(BF16)
    return high, (value - high.astype(F32)).astype(BF16)


def sum_dot(matrix, value):
    first = value.astype(BF16)
    rest = value - first.astype(F32)
    second = rest.astype(BF16)
    third = (rest - second.astype(F32)).astype(BF16)
    return dot_nn(matrix, first) + dot_nn(matrix, second) + dot_nn(matrix, third)


def head_spread(head_count, first_column, columns, head_size):
    row = lax.broadcasted_iota(jnp.int32, (2 * head_count, columns), 0)
    row = jnp.where(row >= head_count, row - head_count, row)
    column = lax.broadcasted_iota(jnp.int32, (2 * head_count, columns), 1) + first_column
    offset = column - row * head_size
    return jnp.where((offset >= 0) & (offset < head_size), 1.0, 0.0).astype(BF16)


def head_collect(head_count, first_column, columns, head_size):
    row = lax.broadcasted_iota(jnp.int32, (columns, head_count), 0) + first_column
    column = lax.broadcasted_iota(jnp.int32, (columns, head_count), 1)
    offset = row - column * head_size
    return jnp.where((offset >= 0) & (offset < head_size), 1.0, 0.0).astype(BF16)


def triangle(rows, lower):
    first = lax.broadcasted_iota(jnp.int32, (rows, rows), 0)
    second = lax.broadcasted_iota(jnp.int32, (rows, rows), 1)
    return (first >= second) if lower else (first <= second)


def start_counts(starts_row):
    rows = starts_row.shape[1]
    flags = starts_row.astype(F32)
    column = jnp.sum(jnp.where(triangle(rows, True), flags, 0.0), axis=1, keepdims=True)
    spread = jnp.broadcast_to(flags, (8, rows)).astype(BF16)
    row = dot_nn(spread, triangle(rows, False).astype(F32).astype(BF16))[:1]
    return column, row


def softplus(value):
    return jnp.maximum(value, 0.0) + jnp.log1p(jnp.exp(-jnp.abs(value)))


def sum_dot_left(value, matrix):
    first = value.astype(BF16)
    rest = value - first.astype(F32)
    second = rest.astype(BF16)
    third = (rest - second.astype(F32)).astype(BF16)
    return dot_nn(first, matrix) + dot_nn(second, matrix) + dot_nn(third, matrix)


def prep_kernel(
    head_size, raw_ref, rate_ref, starts_ref, query_ref, key_ref,
    lead_ref, tail_ref, leadt_ref, tailt_ref, grow_ref, fall_ref, decay_ref, last_ref,
):
    head_count, rows = raw_ref.shape
    step = softplus(raw_ref[...])
    upper = triangle(rows, False).astype(F32).astype(BF16)
    cumulative = sum_dot_left(-step * rate_ref[...], upper)
    count, _ = start_counts(starts_ref[...])
    lead = jnp.where(count == 0.0, query_ref[...].astype(F32), 0.0)
    tail = jnp.where(count == count[rows - 1 :, :], key_ref[...].astype(F32), 0.0)
    lead_ref[...] = lead.astype(BF16)
    tail_ref[...] = tail.astype(BF16)
    leadt_ref[...] = lead.T.astype(BF16)
    tailt_ref[...] = tail.T.astype(BF16)
    fall = jnp.exp(cumulative).T
    fall_ref[...] = jnp.concatenate(halves(fall), axis=1)
    grow_ref[...] = jnp.concatenate(halves((jnp.exp(-cumulative) * step).T), axis=1)
    last = jnp.broadcast_to(fall[rows - 1 :, :], (8, head_count))
    channels = decay_ref.shape[1]
    spread = head_spread(head_count, 0, channels, head_size)
    last_wide = dot_nn(jnp.concatenate(halves(last), axis=1), spread)[:1]
    last_ref[...] = last_wide
    decay_ref[...] = jnp.where(count[rows - 1 :, :] == 0.0, last_wide, 0.0)


def place():
    index = lax.axis_index("seq")
    return (index & 1) == 0, (index & 2) == 0, index >> 2


def joined(first, own_decay, other_decay, own, came):
    one = jnp.ones_like(own_decay)
    forward = (
        jnp.where(first, other_decay, one) * own[0] + jnp.where(first, one, own_decay) * came[0]
    )
    backward = (
        jnp.where(first, one, other_decay) * own[1] + jnp.where(first, own_decay, one) * came[1]
    )
    return forward, backward


def split_pair(first, own_decay, other_decay, own, came, entering, leaving, put_own, put_other):
    @pl.when(first)
    def _():
        put_own(0, entering)
        put_other(0, own_decay * entering + own[0])
        put_other(1, leaving)
        put_own(1, other_decay * leaving + came[1])

    @pl.when(jnp.logical_not(first))
    def _():
        put_other(0, entering)
        put_own(0, other_decay * entering + came[0])
        put_own(1, leaving)
        put_other(1, own_decay * leaving + own[1])


def chip_kernel(
    columns, kept_ref, came_ref, own_ref, other_ref, sent_ref, side_ref, chip_ref=None
):
    first, _, _ = place()
    forward, backward = joined(
        first, own_ref[:, columns], other_ref[:, columns], kept_ref, came_ref
    )
    for chain, value in enumerate((forward, backward)):
        sent_ref[chain] = value[0]
        side_ref[chain] = value[1]
    if chip_ref is not None:
        chip_ref[...] = own_ref[...] * other_ref[...]


def plane_kernel(
    columns, kept_ref, came_ref, own_ref, other_ref, pay_ref, both_ref, plane_ref=None
):
    _, first, plane = place()
    forward, backward = joined(
        first, own_ref[:, columns], other_ref[:, columns], kept_ref, came_ref
    )
    both_ref[0] = forward
    both_ref[1] = backward
    pay_ref[...] = jnp.where((plane & 1) == 1, backward, forward)
    if plane_ref is not None:
        plane_ref[...] = own_ref[...] * other_ref[...]


def absorb(columns, level, plane, taken_refs, others, enter_ref):
    upper = ((plane >> level) & 1) == 1
    taken = taken_refs[0][...]
    for ref in taken_refs[1:]:
        taken = taken + ref[...]
    if level == 0:
        zero = jnp.zeros_like(taken)
        return jnp.where(upper, taken, zero), jnp.where(upper, zero, taken)
    before = after = None
    for lower, ref in enumerate(others[:level]):
        other = ref[:, columns]
        above = ((plane >> lower) & 1) == 1
        one = jnp.ones_like(other)
        first = jnp.where(above, other, one)
        second = jnp.where(above, one, other)
        before = first if before is None else before * first
        after = second if after is None else after * second
    zero = jnp.zeros_like(before)
    return (
        enter_ref[0] + jnp.where(upper, before, zero) * taken,
        enter_ref[1] + jnp.where(upper, zero, after) * taken,
    )


def level_kernel(columns, level, taken_count, *refs):
    taken, refs = refs[:taken_count], refs[taken_count:]
    others, refs = refs[:level], refs[level:]
    enter_ref = None
    if level:
        enter_ref, refs = refs[0], refs[1:]
    both_ref, decay_ref, pay_ref, next_ref = refs
    _, _, plane = place()
    entering, leaving = absorb(columns, level, plane, taken, others, enter_ref)
    next_ref[0] = entering
    next_ref[1] = leaving
    upper = ((plane >> (level + 1)) & 1) == 1
    decay = decay_ref[:, columns]

    @pl.when(upper)
    def _():
        pay_ref[...] = decay * leaving + both_ref[1]

    @pl.when(jnp.logical_not(upper))
    def _():
        pay_ref[...] = decay * entering + both_ref[0]


def top_kernel(columns, level, taken_count, *refs):
    taken, refs = refs[:taken_count], refs[taken_count:]
    others, refs = refs[:level], refs[level:]
    enter_ref = None
    if level:
        enter_ref, refs = refs[0], refs[1:]
    kept_ref, came_ref, own_ref, other_ref, theirs_ref, mine_ref = refs
    _, first, plane = place()
    entering, leaving = absorb(columns, level, plane, taken, others, enter_ref)

    def put_own(chain, value):
        mine_ref[chain] = value

    def put_other(chain, value):
        theirs_ref[chain] = value

    split_pair(
        first, own_ref[:, columns], other_ref[:, columns], kept_ref, came_ref, entering, leaving,
        put_own, put_other,
    )


def device_kernel(
    columns, back_ref, mine_ref, kept_ref, came_ref, own_ref, other_ref, give_ref, stay_ref
):
    first, _, _ = place()
    for slot, source in enumerate((back_ref, mine_ref)):

        def put_own(chain, value, slot=slot):
            stay_ref[chain, slot] = value

        def put_other(chain, value, slot=slot):
            give_ref[chain, slot] = value

        split_pair(
            first, own_ref[:, columns], other_ref[:, columns], kept_ref.at[:, slot],
            came_ref.at[:, slot], source[0], source[1], put_own, put_other,
        )


def states_kernel(
    head_count, head_size, first, in_ref, cot_ref, grow_ref, fall_ref, leadt_ref, tailt_ref,
    last_ref, send_ref, keep_ref,
):
    columns = in_ref.shape[1]
    spread = head_spread(head_count, first + pl.program_id(0) * columns, columns, head_size)
    grown = (dot_nn(grow_ref[...], spread) * in_ref[...].astype(F32)).astype(BF16)
    fallen = (dot_nn(fall_ref[...], spread) * cot_ref[...].astype(F32)).astype(BF16)
    state = dot_nn(tailt_ref[...], grown) * last_ref[...]
    direct = dot_nn(leadt_ref[...], fallen)
    low, mid, _ = place()
    half = state.shape[0] // 2
    quarter = half // 2
    for chain, value in enumerate((state, direct)):
        sent = jnp.where(low, value[half:], value[:half])
        kept = jnp.where(low, value[:half], value[half:])
        for ref, part in ((send_ref, sent), (keep_ref, kept)):
            ref[chain, 0] = jnp.where(mid, part[quarter:], part[:quarter])
            ref[chain, 1] = jnp.where(mid, part[:quarter], part[quarter:])


def scores_kernel(
    head_count, head_size, steps, starts_ref, query_ref, key_ref, in_ref, cot_ref, grow_ref,
    fall_ref, score_ref, scoret_ref, dquery_ref, dkey_ref, total_ref,
):
    columns = in_ref.shape[1]
    rows = in_ref.shape[0]
    step = pl.program_id(0)
    spread = head_spread(head_count, step * columns, columns, head_size)
    grown = (dot_nn(grow_ref[...], spread) * in_ref[...].astype(F32)).astype(BF16)
    fallen = (dot_nn(fall_ref[...], spread) * cot_ref[...].astype(F32)).astype(BF16)
    product = dot_nt(fallen, grown)

    @pl.when(step == 0)
    def _():
        total_ref[...] = product

    @pl.when(step > 0)
    def _():
        total_ref[...] += product

    @pl.when(step == steps - 1)
    def _():
        column, row = start_counts(starts_ref[...])
        same = column == row
        allowed = same & triangle(rows, True)
        score_ref[...] = jnp.where(allowed, dot_nt(query_ref[...], key_ref[...]), 0.0).astype(BF16)
        scoret_ref[...] = jnp.where(
            same & triangle(rows, False), dot_nt(key_ref[...], query_ref[...]), 0.0
        ).astype(BF16)
        grads = jnp.where(allowed, total_ref[...], 0.0)
        dquery_ref[...] = dot_nn(grads.astype(BF16), key_ref[...])
        dkey_ref[...] = dot_nn(grads.T.astype(BF16), query_ref[...])


def arranged(low, mid, took_ref, own_ref, chain):
    parts = []
    for ref in (own_ref, took_ref):
        first = jnp.where(mid, ref[chain, 1], ref[chain, 0])
        second = jnp.where(mid, ref[chain, 0], ref[chain, 1])
        parts.append(jnp.concatenate([first, second], axis=0))
    own, took = parts
    return jnp.concatenate([jnp.where(low, own, took), jnp.where(low, took, own)], axis=0)


def finish_kernel(
    head_count, head_size, first, steps, prior, in_ref, cot_ref, took_ref, own_ref, skip_ref,
    decay_ref, last_ref, grow_ref, fall_ref, lead_ref, tail_ref, score_ref, scoret_ref, starts_ref,
    raw_ref, rate_ref, dquery_in, dkey_in, *refs,
):
    if prior:
        draw_in, refs = refs[0], refs[3:]
    (
        out_ref, din_ref, dquery_ref, dkey_ref, draw_ref,
        rise_ref, sink_ref, edge_ref, dlead_ref, dtail_ref,
    ) = refs
    rows, columns = in_ref.shape
    step = pl.program_id(0)
    start_column = first + step * columns
    low, mid, _ = place()
    entering = arranged(low, mid, took_ref, own_ref, 0)
    leaving = arranged(low, mid, took_ref, own_ref, 1)
    spread = head_spread(head_count, start_column, columns, head_size)
    grow = dot_nn(grow_ref[...], spread)
    fall = dot_nn(fall_ref[...], spread)
    in_wide = in_ref[...].astype(F32)
    cot_wide = cot_ref[...].astype(F32)
    grown = (grow * in_wide).astype(BF16)
    fallen = (fall * cot_wide).astype(BF16)
    entering_bf = entering.astype(BF16)
    leaving_bf = (leaving * last_ref[...]).astype(BF16)

    produced = dot_nn(score_ref[...], grown) + dot_nn(lead_ref[...], entering_bf)
    out_ref[...] = (fall * produced + skip_ref[...] * in_wide).astype(BF16)
    behind = dot_nn(tail_ref[...], leaving_bf)
    pulled = dot_nn(scoret_ref[...], fallen) + behind
    din_ref[...] = (grow * pulled + skip_ref[...] * cot_wide).astype(BF16)

    collect = head_collect(head_count, start_column, columns, head_size)

    def by_head(value):
        return dot_nn(value.astype(BF16), collect)

    grown_wide = grown.astype(F32)
    rise = by_head(fallen.astype(F32) * produced)
    sink = by_head(grown_wide * pulled)
    edge_row = jnp.sum(grown_wide * behind, axis=0, keepdims=True) + decay_ref[...] * jnp.sum(
        entering * leaving, axis=0, keepdims=True
    )
    high, rest = halves(jnp.broadcast_to(edge_row, (8, columns)))
    edge = dot_nn(high, collect) + dot_nn(rest, collect)
    dlead = dot_nt(fallen, entering_bf)
    dtail = dot_nt(grown, leaving_bf)

    @pl.when(step == 0)
    def _():
        rise_ref[...] = rise
        sink_ref[...] = sink
        edge_ref[...] = edge
        dlead_ref[...] = dlead
        dtail_ref[...] = dtail

    @pl.when(step > 0)
    def _():
        rise_ref[...] += rise
        sink_ref[...] += sink
        edge_ref[...] += edge
        dlead_ref[...] += dlead
        dtail_ref[...] += dtail

    @pl.when(step == steps - 1)
    def _():
        count, _ = start_counts(starts_ref[...])
        dquery = dquery_in[...] + jnp.where(count == 0.0, dlead_ref[...], 0.0)
        dkey = dkey_in[...] + jnp.where(count == count[rows - 1 :, :], dtail_ref[...], 0.0)
        dquery_ref[...] = dquery.astype(dquery_ref.dtype)
        dkey_ref[...] = dkey.astype(dkey_ref.dtype)
        upper = triangle(rows, False).astype(F32).astype(BF16)
        later = sum_dot(upper, rise_ref[...] - sink_ref[...]) + edge_ref[:1]
        raw = raw_ref[...]
        dstep = sink_ref[...].T / softplus(raw) - rate_ref[...] * later.T
        draw = dstep / (1.0 + jnp.exp(-raw))
        draw_ref[...] = draw_in[...] + draw if prior else draw


def whole(shape):
    return pl.BlockSpec(shape, lambda i, *_: (0,) * len(shape))


def params():
    return pltpu.CompilerParams(vmem_limit_bytes=VMEM_BYTES)


def cost(flops, count):
    return pl.CostEstimate(flops=flops, bytes_accessed=count, transcendentals=0)


def local(inputs, raw_steps, input_map, output_map, decay_rates, skip_gain, starts, cotangent):
    rows, channels = inputs.shape
    head_count = decay_rates.shape[0]
    head_size = channels // head_count
    state_size = input_map.shape[1]
    width = channels // CHUNKS
    tiles = width // TILE
    quarter = state_size // 4

    size = lax.axis_size("seq")
    planes = size // 4
    levels = planes.bit_length() - 1
    starts_row = starts.reshape(1, rows)
    rate_column = decay_rates.reshape(head_count, 1)
    raw_turned = raw_steps.T
    skip_row = jnp.repeat(skip_gain, head_size).reshape(1, channels)

    def shape(dims, kind=F32):
        return jax.ShapeDtypeStruct(dims, kind)

    lead, tail, leadt, tailt, grow, fall, decay, last = pl.pallas_call(
        functools.partial(prep_kernel, head_size),
        out_shape=(
            shape((rows, state_size), BF16),
            shape((rows, state_size), BF16),
            shape((state_size, rows), BF16),
            shape((state_size, rows), BF16),
            shape((rows, 2 * head_count), BF16),
            shape((rows, 2 * head_count), BF16),
            shape((1, channels)),
            shape((1, channels)),
        ),
        compiler_params=params(),
        name="prep",
    )(raw_turned, rate_column, starts_row, output_map, input_map)

    def pieces(chunk):
        first = chunk * tiles
        tile = pl.BlockSpec((rows, TILE), lambda i, *_: (0, first + i))
        row = pl.BlockSpec((1, TILE), lambda i, *_: (0, first + i))
        part = pl.BlockSpec((2, 2, quarter, TILE), lambda i, *_: (0, 0, 0, i))
        return tile, row, part

    def device_states(chunk):
        tile, row, part = pieces(chunk)
        half = shape((2, 2, quarter, width))
        return pl.pallas_call(
            functools.partial(states_kernel, head_count, head_size, chunk * width),
            out_shape=(half, half),
            grid=(tiles,),
            in_specs=[
                tile, tile, whole(grow.shape), whole(fall.shape), whole(leadt.shape),
                whole(tailt.shape), row,
            ],
            out_specs=(part, part),
            compiler_params=params(),
            cost_estimate=cost(
                4 * rows * state_size * width + 8 * rows * head_count * width, 6 * rows * width
            ),
            name="states",
        )(inputs, cotangent, grow, fall, leadt, tailt, last)

    def swap(value, bit):
        return lax.ppermute(value, "seq", [(i, i ^ bit) for i in range(size)])

    def level_perms(level):
        span = 1 << level
        perms = []
        for shift in range(span):
            pairs = []
            for base in range(0, planes, 2 * span):
                pairs.append((base + span - 1, base + span + shift))
                pairs.append((base + span, base + span - 1 - shift))
            perms.append([(4 * a + r, 4 * b + r) for a, b in pairs for r in range(4)])
        return perms

    def small(kernel, out_shape, name, *operands):
        return pl.pallas_call(
            kernel, out_shape=out_shape, compiler_params=params(), name=name
        )(*operands)

    flat_shape = shape((quarter, width))
    pair_shape = shape((2, quarter, width))
    four_shape = shape((2, 2, quarter, width))
    row_shape = shape((1, channels))
    score_tiles = channels // TILE
    all_tile = pl.BlockSpec((rows, TILE), lambda i, *_: (0, i))

    def scores(input_values):
        square = (rows, rows)
        return pl.pallas_call(
            functools.partial(scores_kernel, head_count, head_size, score_tiles),
            out_shape=(
                shape(square, BF16), shape(square, BF16),
                shape((rows, state_size)), shape((rows, state_size)),
            ),
            grid=(score_tiles,),
            in_specs=[
                whole(starts_row.shape), whole(output_map.shape), whole(input_map.shape),
                all_tile, all_tile, whole(grow.shape), whole(fall.shape),
            ],
            out_specs=(
                whole(square), whole(square),
                whole((rows, state_size)), whole((rows, state_size)),
            ),
            scratch_shapes=[pltpu.VMEM(square, F32)],
            compiler_params=params(),
            cost_estimate=cost(2 * rows * rows * channels, 4 * rows * channels),
            name="scores",
        )(starts_row, output_map, input_map, input_values, cotangent, grow, fall)

    def finish(chunk, took, own, sofar):
        tile, row, part = pieces(chunk)
        square = (rows, rows)
        flat = (rows, state_size)
        by_head = (head_count, rows)
        final = chunk == CHUNKS - 1
        prior = chunk > 0
        out, din, dquery, dkey, draw = sofar
        operands = [
            inputs, cotangent, took, own, skip_row, decay, last, grow, fall, lead, tail,
            score, scoret, starts_row, raw_turned, rate_column, dquery, dkey,
        ]
        in_specs = [
            tile, tile, part, part, row, row, row, whole(grow.shape), whole(fall.shape),
            whole(flat), whole(flat), whole(square), whole(square),
            whole(starts_row.shape), whole(by_head), whole(rate_column.shape),
            whole(flat), whole(flat),
        ]
        aliases = {}
        if prior:
            operands += [draw, out, din]
            in_specs += [whole(by_head), pl.BlockSpec(memory_space=pl.ANY)] + [
                pl.BlockSpec(memory_space=pl.ANY)
            ]
            aliases = {19: 0, 20: 1}
        kind = BF16 if final else F32
        return pl.pallas_call(
            functools.partial(finish_kernel, head_count, head_size, chunk * width, tiles, prior),
            out_shape=(
                shape((rows, channels), BF16), shape((rows, channels), BF16),
                shape(flat, kind), shape(flat, kind), shape(by_head),
            ),
            grid=(tiles,),
            in_specs=in_specs,
            out_specs=(tile, tile, whole(flat), whole(flat), whole(by_head)),
            scratch_shapes=[
                pltpu.VMEM((rows, head_count), F32), pltpu.VMEM((rows, head_count), F32),
                pltpu.VMEM((8, head_count), F32),
                pltpu.VMEM(flat, F32), pltpu.VMEM(flat, F32),
            ],
            input_output_aliases=aliases,
            compiler_params=params(),
            cost_estimate=cost(4 * rows * rows * width, 12 * rows * width),
            name="finish",
        )(*operands)

    every = range(CHUNKS)
    span = [slice(chunk * width, (chunk + 1) * width) for chunk in every]

    sent, kept, came = [None] * CHUNKS, [None] * CHUNKS, [None] * CHUNKS
    decay_other = swap(decay, 1)
    for k in every:
        sent[k], kept[k] = device_states(k)
        came[k] = swap(sent[k], 1)

    side_sent, side_kept, side_came = [None] * CHUNKS, [None] * CHUNKS, [None] * CHUNKS
    for k in every:
        made = small(
            functools.partial(chip_kernel, span[k]),
            (pair_shape, pair_shape) + ((row_shape,) if k == 0 else ()),
            "chip", kept[k], came[k], decay, decay_other,
        )
        side_sent[k], side_kept[k] = made[:2]
        if k == 0:
            chip_decay = made[2]
            chip_other = swap(chip_decay, 2)
        side_came[k] = swap(side_sent[k], 2)

    late = lax.optimization_barrier((inputs, *side_sent))
    score, scoret, dquery, dkey = scores(late[0])
    score, scoret, dquery, dkey, side_came[0] = lax.optimization_barrier(
        (score, scoret, dquery, dkey, side_came[0])
    )

    pay, both = [None] * CHUNKS, [None] * CHUNKS
    others = []
    taken, enter = [None] * CHUNKS, [None] * CHUNKS
    for k in every:
        made = small(
            functools.partial(plane_kernel, span[k]),
            (flat_shape, pair_shape) + ((row_shape,) if k == 0 else ()),
            "plane", side_kept[k], side_came[k], chip_decay, chip_other,
        )
        pay[k], both[k] = made[:2]
        if k == 0:
            plane_decay = group = made[2]
            for level in range(levels - 1):
                other = swap(group, 4 << level)
                others.append(other)
                group = group * other
    for level in range(levels):
        for k in every:
            taken[k] = [lax.ppermute(pay[k], "seq", perm) for perm in level_perms(level)]
        if level == levels - 1:
            break
        for k in every:
            operands = taken[k] + others[:level] + ([enter[k]] if level else [])
            pay[k], enter[k] = small(
                functools.partial(level_kernel, span[k], level, len(taken[k])),
                (flat_shape, pair_shape), "level", *operands, both[k], plane_decay,
            )
    back, mine = [None] * CHUNKS, [None] * CHUNKS
    for k in every:
        operands = taken[k] + others[: levels - 1] + ([enter[k]] if levels > 1 else [])
        theirs, mine[k] = small(
            functools.partial(top_kernel, span[k], levels - 1, len(taken[k])),
            (pair_shape, pair_shape), "top", *operands, side_kept[k], side_came[k],
            chip_decay, chip_other,
        )
        back[k] = swap(theirs, 2)
    took, own = [None] * CHUNKS, [None] * CHUNKS
    for k in every:
        give, own[k] = small(
            functools.partial(device_kernel, span[k]), (four_shape, four_shape), "device",
            back[k], mine[k], kept[k], came[k], decay, decay_other,
        )
        took[k] = swap(give, 1)
    sofar = (None, None, dquery, dkey, None)
    for k in every:
        sofar = finish(k, took[k], own[k], sofar)
    out, din, dquery, dkey, draw = sofar
    return out, din, draw.T, dkey, dquery


def solution(mesh):
    sequence = P(("groups", "seq"), None)
    return jax.shard_map(
        local,
        mesh=mesh,
        in_specs=(
            sequence, sequence, sequence, sequence, P(), P(), P(("groups", "seq")), sequence,
        ),
        out_specs=(sequence,) * 5,
        check_vma=False,
    )
```

```python
import functools

import jax
import jax.numpy as jnp
from jax import lax
from jax.experimental import pallas as pl
from jax.experimental.pallas import tpu as pltpu
from jax.sharding import PartitionSpec as P

CHUNKS = 2
TILE = 640
VMEM_BYTES = 28 * 1024 * 1024

F32 = jnp.float32
BF16 = jnp.bfloat16


def dot_nn(left, right):
    return lax.dot_general(left, right, (((1,), (0,)), ((), ())), preferred_element_type=F32)


def dot_nt(left, right):
    return lax.dot_general(left, right, (((1,), (1,)), ((), ())), preferred_element_type=F32)


def halves(value):
    high = value.astype(BF16)
    return high, (value - high.astype(F32)).astype(BF16)


def sum_dot(matrix, value):
    first = value.astype(BF16)
    rest = value - first.astype(F32)
    second = rest.astype(BF16)
    third = (rest - second.astype(F32)).astype(BF16)
    return dot_nn(matrix, first) + dot_nn(matrix, second) + dot_nn(matrix, third)


def head_spread(depth, offset, head_count, first_column, columns, head_size):
    row = lax.broadcasted_iota(jnp.int32, (depth, columns), 0) - offset
    held = (row >= 0) & (row < 2 * head_count)
    row = jnp.where(row >= head_count, row - head_count, row)
    column = lax.broadcasted_iota(jnp.int32, (depth, columns), 1) + first_column
    inside = column - row * head_size
    return jnp.where(held & (inside >= 0) & (inside < head_size), 1.0, 0.0).astype(BF16)


def head_collect(head_count, first_column, columns, head_size):
    row = lax.broadcasted_iota(jnp.int32, (columns, head_count), 0) + first_column
    column = lax.broadcasted_iota(jnp.int32, (columns, head_count), 1)
    offset = row - column * head_size
    return jnp.where((offset >= 0) & (offset < head_size), 1.0, 0.0).astype(BF16)


def triangle(rows, lower):
    first = lax.broadcasted_iota(jnp.int32, (rows, rows), 0)
    second = lax.broadcasted_iota(jnp.int32, (rows, rows), 1)
    return (first >= second) if lower else (first <= second)


def start_counts(starts_row):
    rows = starts_row.shape[1]
    flags = starts_row.astype(F32)
    column = jnp.sum(jnp.where(triangle(rows, True), flags, 0.0), axis=1, keepdims=True)
    spread = jnp.broadcast_to(flags, (8, rows)).astype(BF16)
    row = dot_nn(spread, triangle(rows, False).astype(F32).astype(BF16))[:1]
    return column, row


def softplus(value):
    return jnp.maximum(value, 0.0) + jnp.log1p(jnp.exp(-jnp.abs(value)))


def sum_dot_left(value, matrix):
    first = value.astype(BF16)
    rest = value - first.astype(F32)
    second = rest.astype(BF16)
    third = (rest - second.astype(F32)).astype(BF16)
    return dot_nn(first, matrix) + dot_nn(second, matrix) + dot_nn(third, matrix)


def fetch(pairs, sems):
    copies = [
        pltpu.make_async_copy(source, target, sems.at[i])
        for i, (source, target) in enumerate(pairs)
    ]
    for copy in copies:
        copy.start()
    return copies


def prep_kernel(
    head_size, raw_hbm, rate_hbm, skip_hbm, starts_hbm, query_hbm, key_hbm,
    heads_ref, maps_ref, turned_ref, rows_ref, decay_ref,
    raw_ref, rate_ref, skip_ref, starts_ref, query_ref, key_ref, sems,
):
    copies = fetch(
        [
            (raw_hbm, raw_ref), (rate_hbm, rate_ref), (skip_hbm, skip_ref),
            (starts_hbm, starts_ref), (query_hbm, query_ref), (key_hbm, key_ref),
        ],
        sems,
    )
    head_count, rows = raw_ref.shape
    upper = triangle(rows, False).astype(F32).astype(BF16)
    for copy in copies:
        copy.wait()
    step = softplus(raw_ref[...])
    rate = jnp.broadcast_to(rate_ref[...], (8, head_count)).T[:, :1]
    cumulative = sum_dot_left(-step * rate, upper)
    count, _ = start_counts(starts_ref[...])
    in_lead = count == 0.0
    in_tail = count == count[rows - 1 :, :]
    state_size = query_ref.shape[1]
    lead = jnp.where(in_lead, query_ref[...].astype(F32), 0.0)
    tail = jnp.where(in_tail, key_ref[...].astype(F32), 0.0)
    maps_ref[:, :state_size] = lead.astype(BF16)
    maps_ref[:, state_size:] = tail.astype(BF16)
    turned_ref[:state_size] = lead.T.astype(BF16)
    turned_ref[state_size:] = tail.T.astype(BF16)
    fall = jnp.exp(cumulative).T
    grow = (jnp.exp(-cumulative) * step).T
    heads_ref[...] = jnp.concatenate(
        halves(fall)
        + halves(grow)
        + (
            jnp.where(in_lead, 1.0, 0.0).astype(BF16),
            jnp.where(in_tail, 1.0, 0.0).astype(BF16),
        ),
        axis=1,
    )
    channels = rows_ref.shape[1]
    spread = head_spread(2 * head_count, 0, head_count, 0, channels, head_size)

    def wide(value):
        return dot_nn(
            jnp.concatenate(halves(jnp.broadcast_to(value, (8, head_count))), axis=1), spread
        )[:1]

    last = wide(fall[rows - 1 :, :])
    decay = jnp.where(count[rows - 1 :, :] == 0.0, last, 0.0)
    rows_ref[0:1, :] = decay
    rows_ref[1:2, :] = last
    rows_ref[2:3, :] = wide(skip_ref[...])
    decay_ref[...] = decay


def place():
    index = lax.axis_index("seq")
    return (index & 1) == 0, (index & 2) == 0, index >> 2


def joined(first, own_decay, other_decay, own, came):
    one = jnp.ones_like(own_decay)
    forward = (
        jnp.where(first, other_decay, one) * own[0] + jnp.where(first, one, own_decay) * came[0]
    )
    backward = (
        jnp.where(first, one, other_decay) * own[1] + jnp.where(first, own_decay, one) * came[1]
    )
    return forward, backward


def split_pair(first, own_decay, other_decay, own, came, entering, leaving, put_own, put_other):
    @pl.when(first)
    def _():
        put_own(0, entering)
        put_other(0, own_decay * entering + own[0])
        put_other(1, leaving)
        put_own(1, other_decay * leaving + came[1])

    @pl.when(jnp.logical_not(first))
    def _():
        put_other(0, entering)
        put_own(0, other_decay * entering + came[0])
        put_own(1, leaving)
        put_other(1, own_decay * leaving + own[1])


def chip_kernel(
    columns, kept_ref, came_ref, own_ref, other_ref, *refs,
):
    if len(refs) > 2:
        chip_ref, chip_other_ref, sent_ref, side_ref, plane_ref = refs
        plane_ref[...] = chip_ref[...] * chip_other_ref[...]
    else:
        sent_ref, side_ref = refs
    first, _, _ = place()
    forward, backward = joined(
        first, own_ref[:, columns], other_ref[:, columns], kept_ref, came_ref
    )
    for chain, value in enumerate((forward, backward)):
        sent_ref[chain] = value[0]
        side_ref[chain] = value[1]


def plane_kernel(columns, kept_ref, came_ref, own_ref, other_ref, pay_ref, both_ref):
    _, first, plane = place()
    forward, backward = joined(
        first, own_ref[:, columns], other_ref[:, columns], kept_ref, came_ref
    )
    both_ref[0] = forward
    both_ref[1] = backward
    pay_ref[...] = jnp.where((plane & 1) == 1, backward, forward)


def absorb(columns, level, plane, taken_refs, others, enter_ref):
    upper = ((plane >> level) & 1) == 1
    taken = taken_refs[0][...]
    for ref in taken_refs[1:]:
        taken = taken + ref[...]
    if level == 0:
        zero = jnp.zeros_like(taken)
        return jnp.where(upper, taken, zero), jnp.where(upper, zero, taken)
    before = after = None
    for lower, ref in enumerate(others[:level]):
        other = ref[:, columns]
        above = ((plane >> lower) & 1) == 1
        one = jnp.ones_like(other)
        first = jnp.where(above, other, one)
        second = jnp.where(above, one, other)
        before = first if before is None else before * first
        after = second if after is None else after * second
    zero = jnp.zeros_like(before)
    return (
        enter_ref[0] + jnp.where(upper, before, zero) * taken,
        enter_ref[1] + jnp.where(upper, zero, after) * taken,
    )


def level_kernel(columns, level, taken_count, *refs):
    taken, refs = refs[:taken_count], refs[taken_count:]
    others, refs = refs[:level], refs[level:]
    enter_ref = None
    if level:
        enter_ref, refs = refs[0], refs[1:]
    both_ref, decay_ref, pay_ref, next_ref = refs
    _, _, plane = place()
    entering, leaving = absorb(columns, level, plane, taken, others, enter_ref)
    next_ref[0] = entering
    next_ref[1] = leaving
    upper = ((plane >> (level + 1)) & 1) == 1
    decay = decay_ref[:, columns]

    @pl.when(upper)
    def _():
        pay_ref[...] = decay * leaving + both_ref[1]

    @pl.when(jnp.logical_not(upper))
    def _():
        pay_ref[...] = decay * entering + both_ref[0]


def top_kernel(columns, level, taken_count, *refs):
    taken, refs = refs[:taken_count], refs[taken_count:]
    others, refs = refs[:level], refs[level:]
    enter_ref = None
    if level:
        enter_ref, refs = refs[0], refs[1:]
    kept_ref, came_ref, own_ref, other_ref, theirs_ref, mine_ref = refs
    _, first, plane = place()
    entering, leaving = absorb(columns, level, plane, taken, others, enter_ref)

    def put_own(chain, value):
        mine_ref[chain] = value

    def put_other(chain, value):
        theirs_ref[chain] = value

    split_pair(
        first, own_ref[:, columns], other_ref[:, columns], kept_ref, came_ref, entering, leaving,
        put_own, put_other,
    )


def device_kernel(
    columns, back_ref, mine_ref, kept_ref, came_ref, own_ref, other_ref, give_ref, stay_ref
):
    first, _, _ = place()
    for slot, source in enumerate((back_ref, mine_ref)):

        def put_own(chain, value, slot=slot):
            stay_ref[chain, slot] = value

        def put_other(chain, value, slot=slot):
            give_ref[chain, slot] = value

        split_pair(
            first, own_ref[:, columns], other_ref[:, columns], kept_ref.at[:, slot],
            came_ref.at[:, slot], source[0], source[1], put_own, put_other,
        )


def scale_columns(heads_ref, head_count, head_size, first, columns):
    heads = heads_ref[...]
    depth = heads.shape[1]
    args = (head_count, first, columns, head_size)
    fall = dot_nn(heads, head_spread(depth, 0, *args))
    grow = dot_nn(heads, head_spread(depth, 2 * head_count, *args))
    return fall, grow


def load_tiles(in_hbm, cot_hbm, in_ref, cot_ref, sems, first, tile):
    found = []
    for i in range(in_ref.shape[1] // tile):
        here = pl.ds(first + i * tile, tile)
        there = pl.ds(i * tile, tile)
        pair = []
        for j, (source, target) in enumerate(((in_hbm, in_ref), (cot_hbm, cot_ref))):
            copy = pltpu.make_async_copy(
                source.at[:, here], target.at[:, there], sems.at[2 * i + j]
            )
            copy.start()
            pair.append(copy)
        found.append(pair)
    return found


def states_kernel(
    head_count, head_size, first_column, tile, in_hbm, cot_hbm, heads_ref, turned_ref, rows_ref,
    send_ref, keep_ref, in_ref, cot_ref, sems,
):
    copies = load_tiles(in_hbm, cot_hbm, in_ref, cot_ref, sems, first_column, tile)
    low, mid, _ = place()
    state_size = turned_ref.shape[0] // 2
    for i, pair in enumerate(copies):
        here = slice(i * tile, (i + 1) * tile)
        there = slice(first_column + i * tile, first_column + (i + 1) * tile)
        fall, grow = scale_columns(heads_ref, head_count, head_size, there.start, tile)
        for copy in pair:
            copy.wait()
        grown = (grow * in_ref[:, here].astype(F32)).astype(BF16)
        fallen = (fall * cot_ref[:, here].astype(F32)).astype(BF16)
        state = dot_nn(turned_ref[state_size:], grown) * rows_ref[1:2, there]
        direct = dot_nn(turned_ref[:state_size], fallen)
        half = state_size // 2
        quarter = half // 2
        for chain, value in enumerate((state, direct)):
            sent = jnp.where(low, value[half:], value[:half])
            kept = jnp.where(low, value[:half], value[half:])
            for ref, part in ((send_ref, sent), (keep_ref, kept)):
                ref[chain, 0, :, here] = jnp.where(mid, part[quarter:], part[:quarter])
                ref[chain, 1, :, here] = jnp.where(mid, part[:quarter], part[quarter:])


def local_kernel(
    head_count, head_size, first_column, tile, initial, final, in_hbm, cot_hbm, heads_ref, rows_ref,
    starts_ref, query_ref, key_ref, *refs,
):
    if not initial:
        score_ref, scoret_ref, total_in, refs = *refs[:3], refs[3:]
    (out_ref, din_ref, grown_ref, fallen_ref, sums_ref), refs = refs[:5], refs[5:]
    if initial:
        (score_ref, scoret_ref), refs = refs[:2], refs[2:]
    (total_out, *key_out), (in_ref, cot_ref, sems) = refs[:-3], refs[-3:]
    copies = load_tiles(in_hbm, cot_hbm, in_ref, cot_ref, sems, first_column, tile)
    rows = in_ref.shape[0]
    if initial or final:
        column, row = start_counts(starts_ref[...])
        same = column == row
        allowed = same & triangle(rows, True)
    if initial:
        score_ref[...] = jnp.where(allowed, dot_nt(query_ref[...], key_ref[...]), 0.0).astype(BF16)
        scoret_ref[...] = jnp.where(
            same & triangle(rows, False), dot_nt(key_ref[...], query_ref[...]), 0.0
        ).astype(BF16)
    total = None if initial else total_in[...]
    rise = sink = None
    for i, pair in enumerate(copies):
        here = slice(i * tile, (i + 1) * tile)
        there = slice(first_column + i * tile, first_column + (i + 1) * tile)
        fall, grow = scale_columns(heads_ref, head_count, head_size, there.start, tile)
        collect = head_collect(head_count, there.start, tile, head_size)
        for copy in pair:
            copy.wait()
        in_wide = in_ref[:, here].astype(F32)
        cot_wide = cot_ref[:, here].astype(F32)
        skip = rows_ref[2:3, there]
        grown = (grow * in_wide).astype(BF16)
        fallen = (fall * cot_wide).astype(BF16)
        grown_ref[:, here] = grown
        fallen_ref[:, here] = fallen
        product = dot_nt(fallen, grown)
        total = product if total is None else total + product
        produced = dot_nn(score_ref[...], grown)
        out_ref[:, here] = fall * produced + skip * in_wide
        rise_now = dot_nn((fallen.astype(F32) * produced).astype(BF16), collect)
        pulled = dot_nn(scoret_ref[...], fallen)
        din_ref[:, here] = grow * pulled + skip * cot_wide
        sink_now = dot_nn((grown.astype(F32) * pulled).astype(BF16), collect)
        rise = rise_now if rise is None else rise + rise_now
        sink = sink_now if sink is None else sink + sink_now
    sums_ref[0] = rise
    sums_ref[1] = sink
    if final:
        grads = jnp.where(allowed, total, 0.0)
        total_out[...] = dot_nn(grads.astype(BF16), key_ref[...])
        key_out[0][...] = dot_nn(grads.T.astype(BF16), query_ref[...])
    else:
        total_out[...] = total


def arranged(low, mid, took_ref, own_ref, chain):
    parts = []
    for ref in (own_ref, took_ref):
        first = jnp.where(mid, ref[chain, 1], ref[chain, 0])
        second = jnp.where(mid, ref[chain, 0], ref[chain, 1])
        parts.append(jnp.concatenate([first, second], axis=0))
    own, took = parts
    return jnp.concatenate([jnp.where(low, own, took), jnp.where(low, took, own)], axis=0)


def finish_kernel(
    head_count, head_size, first_column, steps, prior, local_out_ref, local_din_ref, grown_ref,
    fallen_ref, took_ref, own_ref, rows_ref, heads_ref, maps_ref, sums_ref, raw_ref, rate_ref,
    dquery_in, dkey_in, *refs,
):
    if prior:
        draw_in, refs = refs[0], refs[3:]
    out_ref, din_ref, dquery_ref, dkey_ref, draw_ref, rise_ref, sink_ref, edge_ref, dmap_ref = refs
    rows, columns = grown_ref.shape
    state_size = maps_ref.shape[1] // 2
    step = pl.program_id(0)
    start_column = first_column + step * columns
    low, mid, _ = place()
    entering = arranged(low, mid, took_ref, own_ref, 0)
    leaving = arranged(low, mid, took_ref, own_ref, 1)
    fall, grow = scale_columns(heads_ref, head_count, head_size, start_column, columns)
    grown = grown_ref[...]
    fallen = fallen_ref[...]
    entering_bf = entering.astype(BF16)
    leaving_bf = (leaving * rows_ref[1:2, :]).astype(BF16)
    reached = dot_nn(maps_ref[:, :state_size], entering_bf)
    behind = dot_nn(maps_ref[:, state_size:], leaving_bf)
    out_ref[...] = (local_out_ref[...] + fall * reached).astype(BF16)
    din_ref[...] = (local_din_ref[...] + grow * behind).astype(BF16)
    collect = head_collect(head_count, start_column, columns, head_size)
    rise = dot_nn((fallen.astype(F32) * reached).astype(BF16), collect)
    pulled = grown.astype(F32) * behind
    sink = dot_nn(pulled.astype(BF16), collect)
    edge_row = jnp.sum(pulled, axis=0, keepdims=True) + rows_ref[0:1, :] * jnp.sum(
        entering * leaving, axis=0, keepdims=True
    )
    high, rest = halves(jnp.broadcast_to(edge_row, (8, columns)))
    edge = dot_nn(high, collect) + dot_nn(rest, collect)
    dlead = dot_nt(fallen, entering_bf)
    dtail = dot_nt(grown, leaving_bf)

    @pl.when(step == 0)
    def _():
        rise_ref[...] = sums_ref[0] + rise
        sink_ref[...] = sums_ref[1] + sink
        edge_ref[...] = edge
        dmap_ref[:, :state_size] = dlead
        dmap_ref[:, state_size:] = dtail

    @pl.when(step > 0)
    def _():
        rise_ref[...] += rise
        sink_ref[...] += sink
        edge_ref[...] += edge
        dmap_ref[:, :state_size] += dlead
        dmap_ref[:, state_size:] += dtail

    @pl.when(step == steps - 1)
    def _():
        in_lead = heads_ref[:, 4 * head_count : 4 * head_count + 1].astype(F32) > 0.5
        in_tail = heads_ref[:, 4 * head_count + 1 : 4 * head_count + 2].astype(F32) > 0.5
        dquery_ref[...] = (
            dquery_in[...] + jnp.where(in_lead, dmap_ref[:, :state_size], 0.0)
        ).astype(dquery_ref.dtype)
        dkey_ref[...] = (
            dkey_in[...] + jnp.where(in_tail, dmap_ref[:, state_size:], 0.0)
        ).astype(dkey_ref.dtype)
        lower = triangle(rows, True).astype(F32).astype(BF16)
        sink_turned = sink_ref[...].T
        later = sum_dot_left(rise_ref[...].T - sink_turned, lower) + edge_ref[...].T[:, :1]
        raw = raw_ref[...]
        rate = jnp.broadcast_to(rate_ref[...], (8, head_count)).T[:, :1]
        draw = (sink_turned / softplus(raw) - rate * later) / (1.0 + jnp.exp(-raw))
        draw_ref[...] = draw_in[...] + draw if prior else draw


def whole(shape):
    return pl.BlockSpec(shape, lambda i, *_: (0,) * len(shape))


def params():
    return pltpu.CompilerParams(vmem_limit_bytes=VMEM_BYTES)


def cost(flops, count):
    return pl.CostEstimate(flops=flops, bytes_accessed=count, transcendentals=0)


HBM = pl.BlockSpec(memory_space=pltpu.HBM)
NEAR = pl.BlockSpec(memory_space=pltpu.VMEM)


def local(inputs, raw_steps, input_map, output_map, decay_rates, skip_gain, starts, cotangent):
    rows, channels = inputs.shape
    head_count = decay_rates.shape[0]
    head_size = channels // head_count
    state_size = input_map.shape[1]
    width = channels // CHUNKS
    tiles = width // TILE
    quarter = state_size // 4

    size = lax.axis_size("seq")
    planes = size // 4
    levels = planes.bit_length() - 1
    starts_row = starts.reshape(1, rows)
    rate_row = decay_rates.reshape(1, head_count)
    skip_heads = skip_gain.reshape(1, head_count)
    raw_turned = raw_steps.T

    def far(value):
        return pltpu.with_memory_space_constraint(value, pltpu.HBM)

    def shape(dims, kind=F32):
        return jax.ShapeDtypeStruct(dims, kind)

    heads, maps, turned, wide_rows, decay = pl.pallas_call(
        functools.partial(prep_kernel, head_size),
        out_shape=(
            shape((rows, 4 * head_count + 2), BF16),
            shape((rows, 2 * state_size), BF16),
            shape((2 * state_size, rows), BF16),
            shape((8, channels)),
            shape((1, channels)),
        ),
        in_specs=[HBM] * 6,
        scratch_shapes=[
            pltpu.VMEM((head_count, rows), F32), pltpu.VMEM((1, head_count), F32),
            pltpu.VMEM((1, head_count), F32), pltpu.VMEM((1, rows), jnp.int32),
            pltpu.VMEM((rows, state_size), BF16), pltpu.VMEM((rows, state_size), BF16),
            pltpu.SemaphoreType.DMA((6,)),
        ],
        compiler_params=params(),
        name="prep",
    )(*(far(v) for v in (raw_turned, rate_row, skip_heads, starts_row, output_map, input_map)))

    flat_shape = shape((quarter, width))
    pair_shape = shape((2, quarter, width))
    four_shape = shape((2, 2, quarter, width))
    row_shape = shape((1, channels))
    tile_scratch = [
        pltpu.VMEM((rows, width), BF16), pltpu.VMEM((rows, width), BF16),
        pltpu.SemaphoreType.DMA((2 * tiles,)),
    ]

    def device_states(chunk, rows_value):
        return pl.pallas_call(
            functools.partial(states_kernel, head_count, head_size, chunk * width, TILE),
            out_shape=(four_shape, four_shape),
            in_specs=[HBM, HBM, NEAR, NEAR, NEAR],
            scratch_shapes=tile_scratch,
            compiler_params=params(),
            cost_estimate=cost(1000, 1000),
            name="states",
        )(far(inputs), far(cotangent), heads, turned, rows_value)

    def swap(value, bit):
        return lax.ppermute(value, "seq", [(i, i ^ bit) for i in range(size)])

    def level_perms(level):
        span = 1 << level
        perms = []
        for shift in range(span):
            pairs = []
            for base in range(0, planes, 2 * span):
                pairs.append((base + span - 1, base + span + shift))
                pairs.append((base + span, base + span - 1 - shift))
            perms.append([(4 * a + r, 4 * b + r) for a, b in pairs for r in range(4)])
        return perms

    def small(kernel, out_shape, name, *operands):
        return pl.pallas_call(
            kernel, out_shape=out_shape, compiler_params=params(), name=name
        )(*operands)

    def block_parts(chunk, heads_value, sofar):
        initial = chunk == 0
        final = chunk == CHUNKS - 1
        square = (rows, rows)
        block = (rows, width)
        outs = [
            shape(block), shape(block), shape(block, BF16), shape(block, BF16),
            shape((2, rows, head_count)),
        ]
        if initial:
            outs += [shape(square, BF16), shape(square, BF16)]
        outs += [shape((rows, state_size))] * 2 if final else [shape(square)]
        operands = [
            far(inputs), far(cotangent), heads_value, wide_rows, starts_row, output_map, input_map,
        ] + list(sofar)
        made = pl.pallas_call(
            functools.partial(
                local_kernel, head_count, head_size, chunk * width, TILE, initial, final
            ),
            out_shape=tuple(outs),
            in_specs=[HBM, HBM] + [NEAR] * (len(operands) - 2),
            scratch_shapes=tile_scratch,
            compiler_params=params(),
            cost_estimate=cost(1000, 1000),
            name="block",
        )(*operands)
        if final:
            return made[:5], tuple(made[-2:])
        if initial:
            return made[:5], tuple(made[5:])
        return made[:5], (sofar[0], sofar[1], made[5])

    def finish(chunk, block, took, own, grads, prior):
        tile = pl.BlockSpec((rows, TILE), lambda i: (0, i))
        placed = pl.BlockSpec((rows, TILE), lambda i: (0, chunk * tiles + i))
        row = pl.BlockSpec((8, TILE), lambda i: (0, chunk * tiles + i))
        part = pl.BlockSpec((2, 2, quarter, TILE), lambda i: (0, 0, 0, i))
        flat = (rows, state_size)
        by_head = (head_count, rows)
        operands = [
            *block[:4], took, own, wide_rows, heads, maps, block[4], raw_turned, rate_row, *grads,
        ]
        in_specs = [
            tile, tile, tile, tile, part, part, row, whole(heads.shape), whole(maps.shape),
            whole(block[4].shape), whole(by_head), whole(rate_row.shape), whole(flat), whole(flat),
        ]
        aliases = {}
        if prior:
            operands += list(prior)
            in_specs += [whole(by_head)] + [pl.BlockSpec(memory_space=pl.ANY)] * 2
            aliases = {15: 0, 16: 1}
        kind = BF16 if chunk == CHUNKS - 1 else F32
        return pl.pallas_call(
            functools.partial(
                finish_kernel, head_count, head_size, chunk * width, tiles, bool(prior)
            ),
            out_shape=(
                shape((rows, channels), BF16), shape((rows, channels), BF16),
                shape(flat, kind), shape(flat, kind), shape(by_head),
            ),
            grid=(tiles,),
            in_specs=in_specs,
            out_specs=(placed, placed, whole(flat), whole(flat), whole(by_head)),
            scratch_shapes=[
                pltpu.VMEM((rows, head_count), F32), pltpu.VMEM((rows, head_count), F32),
                pltpu.VMEM((8, head_count), F32), pltpu.VMEM((rows, 2 * state_size), F32),
            ],
            input_output_aliases=aliases,
            compiler_params=params(),
            cost_estimate=cost(1000, 1000),
            name="finish",
        )(*operands)

    every = range(CHUNKS)
    span = [slice(chunk * width, (chunk + 1) * width) for chunk in every]
    tie = lax.optimization_barrier

    sent, kept, came = [None] * CHUNKS, [None] * CHUNKS, [None] * CHUNKS
    decay_other = swap(decay, 1)
    rows_now = wide_rows
    for k in every:
        sent[k], kept[k] = device_states(k, rows_now)
        came[k] = swap(sent[k], 1)
        if k == 0:
            ready = tie((decay_other, sent[0]))
            chip_decay = decay * ready[0]
            chip_other = swap(chip_decay, 2)
            rows_now = tie((wide_rows, chip_decay))[0]

    order = [sent[-1]]

    def follow(value):
        return tie((value, order[0]))[0]

    side_sent, side_kept, side_came = [None] * CHUNKS, [None] * CHUNKS, [None] * CHUNKS
    for k in every:
        made = small(
            functools.partial(chip_kernel, span[k]),
            (pair_shape, pair_shape) + ((row_shape,) if k == 0 else ()),
            "chip", follow(kept[k]), came[k], decay, decay_other,
            *((chip_decay, chip_other) if k == 0 else ()),
        )
        side_sent[k], side_kept[k] = made[:2]
        order[0] = side_sent[k]
        if k == 0:
            plane_decay = group = made[2]
            others = []
            for level in range(levels - 1):
                other = swap(group, 4 << level)
                others.append(other)
                group = group * other
        side_came[k] = swap(side_sent[k], 2)

    blocks = [None] * CHUNKS
    blocks[0], sofar = block_parts(0, follow(heads), ())
    order[0] = sofar[0]

    pay, both = [None] * CHUNKS, [None] * CHUNKS
    taken, enter = [None] * CHUNKS, [None] * CHUNKS
    for k in every:
        pay[k], both[k] = small(
            functools.partial(plane_kernel, span[k]), (flat_shape, pair_shape), "plane",
            follow(side_kept[k]), side_came[k], chip_decay, chip_other,
        )
        order[0] = pay[k]
        taken[k] = [lax.ppermute(pay[k], "seq", perm) for perm in level_perms(0)]
        if k + 1 < CHUNKS:
            blocks[k + 1], sofar = block_parts(k + 1, follow(heads), sofar)
            order[0] = blocks[k + 1][4]
    for level in range(levels - 1):
        for k in every:
            operands = taken[k] + others[:level] + ([enter[k]] if level else [])
            pay[k], enter[k] = small(
                functools.partial(level_kernel, span[k], level, len(taken[k])),
                (flat_shape, pair_shape), "level", *operands, follow(both[k]), plane_decay,
            )
            order[0] = pay[k]
            taken[k] = [lax.ppermute(pay[k], "seq", perm) for perm in level_perms(level + 1)]
    back, mine = [None] * CHUNKS, [None] * CHUNKS
    for k in every:
        operands = taken[k] + others[: levels - 1] + ([enter[k]] if levels > 1 else [])
        theirs, mine[k] = small(
            functools.partial(top_kernel, span[k], levels - 1, len(taken[k])),
            (pair_shape, pair_shape), "top", *operands, follow(side_kept[k]), side_came[k],
            chip_decay, chip_other,
        )
        order[0] = theirs
        back[k] = swap(theirs, 2)
    prior = ()
    grads = sofar
    for k in every:
        give, own = small(
            functools.partial(device_kernel, span[k]), (four_shape, four_shape), "device",
            back[k], follow(mine[k]), kept[k], came[k], decay, decay_other,
        )
        took = swap(give, 1)
        out, din, dquery, dkey, draw = finish(k, blocks[k], took, own, grads, prior)
        grads = (dquery, dkey)
        order[0] = draw
        prior = (draw, out, din)
    return out, din, draw.T, dkey, dquery


def solution(mesh):
    sequence = P(("groups", "seq"), None)
    return jax.shard_map(
        local,
        mesh=mesh,
        in_specs=(
            sequence, sequence, sequence, sequence, P(), P(), P(("groups", "seq")), sequence,
        ),
        out_specs=(sequence,) * 5,
        check_vma=False,
    )
```

```python
import functools

import jax
import jax.numpy as jnp
from jax import lax
from jax.experimental import pallas as pl
from jax.experimental.pallas import tpu as pltpu
from jax.sharding import PartitionSpec as P

WIDTHS = (10, 10)
TILES = (5, 5)
SLACK = 1.0
SMALL_COST = 900_000_000
STATES_COST = 4_000_000_000
VMEM_BYTES = 28 * 1024 * 1024

F32 = jnp.float32
BF16 = jnp.bfloat16


def dot_nn(left, right):
    return lax.dot_general(left, right, (((1,), (0,)), ((), ())), preferred_element_type=F32)


def dot_nt(left, right):
    return lax.dot_general(left, right, (((1,), (1,)), ((), ())), preferred_element_type=F32)


def halves(value):
    high = value.astype(BF16)
    return high, (value - high.astype(F32)).astype(BF16)


def sum_dot(matrix, value):
    first = value.astype(BF16)
    rest = value - first.astype(F32)
    second = rest.astype(BF16)
    third = (rest - second.astype(F32)).astype(BF16)
    return dot_nn(matrix, first) + dot_nn(matrix, second) + dot_nn(matrix, third)


def head_spread(depth, offset, head_count, first_column, columns, head_size):
    row = lax.broadcasted_iota(jnp.int32, (depth, columns), 0) - offset
    held = (row >= 0) & (row < 2 * head_count)
    row = jnp.where(row >= head_count, row - head_count, row)
    column = lax.broadcasted_iota(jnp.int32, (depth, columns), 1) + first_column
    inside = column - row * head_size
    return jnp.where(held & (inside >= 0) & (inside < head_size), 1.0, 0.0).astype(BF16)


def head_collect(head_count, first_column, columns, head_size):
    row = lax.broadcasted_iota(jnp.int32, (columns, head_count), 0) + first_column
    column = lax.broadcasted_iota(jnp.int32, (columns, head_count), 1)
    offset = row - column * head_size
    return jnp.where((offset >= 0) & (offset < head_size), 1.0, 0.0).astype(BF16)


def triangle(rows, lower):
    first = lax.broadcasted_iota(jnp.int32, (rows, rows), 0)
    second = lax.broadcasted_iota(jnp.int32, (rows, rows), 1)
    return (first >= second) if lower else (first <= second)


def start_counts(starts_row):
    rows = starts_row.shape[1]
    flags = starts_row.astype(F32)
    column = jnp.sum(jnp.where(triangle(rows, True), flags, 0.0), axis=1, keepdims=True)
    spread = jnp.broadcast_to(flags, (8, rows)).astype(BF16)
    row = dot_nn(spread, triangle(rows, False).astype(F32).astype(BF16))[:1]
    return column, row


def softplus(value):
    return jnp.maximum(value, 0.0) + jnp.log1p(jnp.exp(-jnp.abs(value)))


def sum_dot_left(value, matrix):
    first = value.astype(BF16)
    rest = value - first.astype(F32)
    second = rest.astype(BF16)
    third = (rest - second.astype(F32)).astype(BF16)
    return dot_nn(first, matrix) + dot_nn(second, matrix) + dot_nn(third, matrix)


def fetch(pairs, sems):
    copies = [
        pltpu.make_async_copy(source, target, sems.at[i])
        for i, (source, target) in enumerate(pairs)
    ]
    for copy in copies:
        copy.start()
    return copies


def prep_kernel(
    head_size, raw_hbm, rate_hbm, skip_hbm, starts_hbm, query_hbm, key_hbm,
    heads_ref, maps_ref, turned_ref, rows_ref, decay_ref,
    raw_ref, rate_ref, skip_ref, starts_ref, query_ref, key_ref, sems,
):
    copies = fetch(
        [
            (raw_hbm, raw_ref), (rate_hbm, rate_ref), (skip_hbm, skip_ref),
            (starts_hbm, starts_ref), (query_hbm, query_ref), (key_hbm, key_ref),
        ],
        sems,
    )
    head_count, rows = raw_ref.shape
    upper = triangle(rows, False).astype(F32).astype(BF16)
    for copy in copies:
        copy.wait()
    step = softplus(raw_ref[...])
    rate = jnp.broadcast_to(rate_ref[...], (8, head_count)).T[:, :1]
    cumulative = sum_dot_left(-step * rate, upper)
    count, _ = start_counts(starts_ref[...])
    in_lead = count == 0.0
    in_tail = count == count[rows - 1 :, :]
    state_size = query_ref.shape[1]
    lead = jnp.where(in_lead, query_ref[...].astype(F32), 0.0)
    tail = jnp.where(in_tail, key_ref[...].astype(F32), 0.0)
    maps_ref[:, :state_size] = lead.astype(BF16)
    maps_ref[:, state_size:] = tail.astype(BF16)
    turned_ref[:state_size] = lead.T.astype(BF16)
    turned_ref[state_size:] = tail.T.astype(BF16)
    fall = jnp.exp(cumulative).T
    grow = (jnp.exp(-cumulative) * step).T
    heads_ref[...] = jnp.concatenate(
        halves(fall)
        + halves(grow)
        + (
            jnp.where(in_lead, 1.0, 0.0).astype(BF16),
            jnp.where(in_tail, 1.0, 0.0).astype(BF16),
        ),
        axis=1,
    )
    channels = rows_ref.shape[1]
    spread = head_spread(2 * head_count, 0, head_count, 0, channels, head_size)

    def wide(value):
        return dot_nn(
            jnp.concatenate(halves(jnp.broadcast_to(value, (8, head_count))), axis=1), spread
        )[:1]

    last = wide(fall[rows - 1 :, :])
    decay = jnp.where(count[rows - 1 :, :] == 0.0, last, 0.0)
    rows_ref[0:1, :] = decay
    rows_ref[1:2, :] = last
    rows_ref[2:3, :] = wide(skip_ref[...])
    decay_ref[...] = decay


def place():
    index = lax.axis_index("seq")
    return ((index & 1) == 0, (index & 2) == 0, (index & 4) == 0), index >> 3


def outward(firsts, value):
    half = value.shape[0] // 2
    low, high = value[:half], value[half:]
    other, own = jnp.where(firsts[0], high, low), jnp.where(firsts[0], low, high)
    if len(firsts) > 1:
        other, own = outward(firsts[1:], other), outward(firsts[1:], own)
    return jnp.concatenate([other, own], axis=0)


def inward(firsts, other, own):
    if len(firsts) > 1:
        half = own.shape[0] // 2
        other = inward(firsts[1:], other[:half], other[half:])
        own = inward(firsts[1:], own[:half], own[half:])
    low, high = jnp.where(firsts[0], own, other), jnp.where(firsts[0], other, own)
    return jnp.concatenate([low, high], axis=0)


def joined(first, own_decay, other_decay, own, came):
    one = jnp.ones_like(own_decay)
    forward = (
        jnp.where(first, other_decay, one) * own[0] + jnp.where(first, one, own_decay) * came[0]
    )
    backward = (
        jnp.where(first, one, other_decay) * own[1] + jnp.where(first, own_decay, one) * came[1]
    )
    return forward, backward


def split_pair(first, own_decay, other_decay, own, came, entering, leaving, put_own, put_other):
    @pl.when(first)
    def _():
        put_own(0, entering)
        put_other(0, own_decay * entering + own(0))
        put_other(1, leaving)
        put_own(1, other_decay * leaving + came(1))

    @pl.when(jnp.logical_not(first))
    def _():
        put_other(0, entering)
        put_own(0, other_decay * entering + came(0))
        put_own(1, leaving)
        put_other(1, own_decay * leaving + own(1))


def join_kernel(columns, level, kept_ref, came_ref, own_ref, other_ref, sent_ref, next_ref=None):
    firsts, unit = place()
    forward, backward = joined(
        firsts[level], own_ref[:, columns], other_ref[:, columns], kept_ref, came_ref
    )
    if level == 2:
        if next_ref is not None:
            next_ref[0] = forward
            next_ref[1] = backward
        sent_ref[...] = jnp.where((unit & 1) == 1, backward, forward)
        return
    half = forward.shape[0] // 2
    for chain, value in enumerate((forward, backward)):
        sent_ref[chain] = value[:half]
        next_ref[chain] = value[half:]


def absorb(columns, level, plane, taken_refs, others, enter_ref):
    upper = ((plane >> level) & 1) == 1
    taken = taken_refs[0][...]
    for ref in taken_refs[1:]:
        taken = taken + ref[...]
    if level == 0:
        zero = jnp.zeros_like(taken)
        return jnp.where(upper, taken, zero), jnp.where(upper, zero, taken)
    before = after = None
    for lower, ref in enumerate(others[:level]):
        other = ref[:, columns]
        above = ((plane >> lower) & 1) == 1
        one = jnp.ones_like(other)
        first = jnp.where(above, other, one)
        second = jnp.where(above, one, other)
        before = first if before is None else before * first
        after = second if after is None else after * second
    zero = jnp.zeros_like(before)
    return (
        enter_ref[0] + jnp.where(upper, before, zero) * taken,
        enter_ref[1] + jnp.where(upper, zero, after) * taken,
    )


def level_kernel(columns, level, taken_count, *refs):
    taken, refs = refs[:taken_count], refs[taken_count:]
    others, refs = refs[:level], refs[level:]
    enter_ref = None
    if level:
        enter_ref, refs = refs[0], refs[1:]
    both_ref, decay_ref, pay_ref, next_ref = refs
    _, plane = place()
    entering, leaving = absorb(columns, level, plane, taken, others, enter_ref)
    next_ref[0] = entering
    next_ref[1] = leaving
    upper = ((plane >> (level + 1)) & 1) == 1
    decay = decay_ref[:, columns]

    @pl.when(upper)
    def _():
        pay_ref[...] = decay * leaving + both_ref[1]

    @pl.when(jnp.logical_not(upper))
    def _():
        pay_ref[...] = decay * entering + both_ref[0]


def top_kernel(columns, level, taken_count, *refs):
    taken, refs = refs[:taken_count], refs[taken_count:]
    others, refs = refs[:level], refs[level:]
    enter_ref = None
    if level:
        enter_ref, refs = refs[0], refs[1:]
    kept_ref, came_ref, own_ref, other_ref, theirs_ref, mine_ref = refs
    firsts, plane = place()
    entering, leaving = absorb(columns, level, plane, taken, others, enter_ref)

    def put_own(chain, value):
        mine_ref[chain] = value

    def put_other(chain, value):
        theirs_ref[chain] = value

    split_pair(
        firsts[2], own_ref[:, columns], other_ref[:, columns], lambda i: kept_ref[i],
        lambda i: came_ref[i], entering, leaving, put_own, put_other,
    )


def return_kernel(
    columns, level, back_ref, mine_ref, kept_ref, came_ref, own_ref, other_ref, give_ref, stay_ref
):
    first = place()[0][level]
    half = back_ref.shape[1]
    for slot, source in enumerate((back_ref, mine_ref)):
        here = slice(slot * half, (slot + 1) * half)

        def put_own(chain, value, here=here):
            stay_ref[chain, here] = value

        def put_other(chain, value, here=here):
            give_ref[chain, here] = value

        split_pair(
            first, own_ref[:, columns], other_ref[:, columns],
            lambda i, here=here: kept_ref[i, here], lambda i, here=here: came_ref[i, here],
            source[0], source[1], put_own, put_other,
        )


def scale_columns(heads_ref, head_count, head_size, first, columns):
    heads = heads_ref[...]
    depth = heads.shape[1]
    args = (head_count, first, columns, head_size)
    fall = dot_nn(heads, head_spread(depth, 0, *args))
    grow = dot_nn(heads, head_spread(depth, 2 * head_count, *args))
    return fall, grow


def load_tiles(in_hbm, cot_hbm, in_ref, cot_ref, sems, first, tile):
    found = []
    for i in range(in_ref.shape[1] // tile):
        here = pl.ds(first + i * tile, tile)
        there = pl.ds(i * tile, tile)
        pair = []
        for j, (source, target) in enumerate(((in_hbm, in_ref), (cot_hbm, cot_ref))):
            copy = pltpu.make_async_copy(
                source.at[:, here], target.at[:, there], sems.at[2 * i + j]
            )
            copy.start()
            pair.append(copy)
        found.append(pair)
    return found


def states_kernel(
    head_count, head_size, first_column, tile, in_hbm, cot_hbm, heads_ref, turned_ref, rows_ref,
    send_ref, keep_ref, in_ref, cot_ref, sems,
):
    copies = load_tiles(in_hbm, cot_hbm, in_ref, cot_ref, sems, first_column, tile)
    firsts, _ = place()
    state_size = turned_ref.shape[0] // 2
    for i, pair in enumerate(copies):
        here = slice(i * tile, (i + 1) * tile)
        there = slice(first_column + i * tile, first_column + (i + 1) * tile)
        fall, grow = scale_columns(heads_ref, head_count, head_size, there.start, tile)
        for copy in pair:
            copy.wait()
        grown = (grow * in_ref[:, here].astype(F32)).astype(BF16)
        fallen = (fall * cot_ref[:, here].astype(F32)).astype(BF16)
        state = dot_nn(turned_ref[state_size:], grown) * rows_ref[1:2, there]
        direct = dot_nn(turned_ref[:state_size], fallen)
        half = state_size // 2
        for chain, value in enumerate((state, direct)):
            value = outward(firsts, value)
            send_ref[chain, :, here] = value[:half]
            keep_ref[chain, :, here] = value[half:]


def local_kernel(
    head_count, head_size, first_column, initial, final, in_hbm, cot_hbm, heads_ref, rows_ref,
    starts_ref, query_ref, key_ref, *refs,
):
    if not initial:
        score_ref, scoret_ref, total_in, refs = *refs[:3], refs[3:]
    out_ref, din_ref, grown_ref, fallen_ref, grow_ref, fall_ref, sums_ref = refs[:7]
    refs = refs[7:]
    if initial:
        (score_ref, scoret_ref), refs = refs[:2], refs[2:]
    (total_out, *key_out), (in_ref, cot_ref, sems) = refs[:-3], refs[-3:]
    rows, columns = in_ref.shape
    ((in_copy, cot_copy),) = load_tiles(
        in_hbm, cot_hbm, in_ref, cot_ref, sems, first_column, columns
    )
    if initial or final:
        column, row = start_counts(starts_ref[...])
        same = column == row
        allowed = same & triangle(rows, True)
    if initial:
        score_ref[...] = jnp.where(allowed, dot_nt(query_ref[...], key_ref[...]), 0.0).astype(BF16)
        scoret_ref[...] = jnp.where(
            same & triangle(rows, False), dot_nt(key_ref[...], query_ref[...]), 0.0
        ).astype(BF16)
    fall, grow = scale_columns(heads_ref, head_count, head_size, first_column, columns)
    fall_ref[...] = fall.astype(BF16)
    grow_ref[...] = grow.astype(BF16)
    collect = head_collect(head_count, first_column, columns, head_size)
    in_copy.wait()
    cot_copy.wait()
    in_wide = in_ref[...].astype(F32)
    cot_wide = cot_ref[...].astype(F32)
    skip = rows_ref[2:3, first_column : first_column + columns]
    grown = (grow * in_wide).astype(BF16)
    fallen = (fall * cot_wide).astype(BF16)
    grown_ref[...] = grown
    fallen_ref[...] = fallen
    total = dot_nt(fallen, grown)
    if not initial:
        total += total_in[...]
    produced = dot_nn(score_ref[...], grown)
    out_ref[...] = fall * produced + skip * in_wide
    sums_ref[0] = dot_nn((fallen.astype(F32) * produced).astype(BF16), collect)
    pulled = dot_nn(scoret_ref[...], fallen)
    din_ref[...] = grow * pulled + skip * cot_wide
    sums_ref[1] = dot_nn((grown.astype(F32) * pulled).astype(BF16), collect)
    if final:
        grads = jnp.where(allowed, total, 0.0)
        total_out[...] = dot_nn(grads.astype(BF16), key_ref[...])
        key_out[0][...] = dot_nn(grads.T.astype(BF16), query_ref[...])
    else:
        total_out[...] = total


def finish_kernel(
    head_count, head_size, first_column, tile, pieces, prior, final, *refs,
):
    blocks = [refs[7 * i : 7 * i + 7] for i in range(pieces)]
    (took_ref, own_ref, rows_ref, heads_ref, maps_ref, dquery_in, dkey_in) = refs[
        7 * pieces : 7 * pieces + 7
    ]
    refs = refs[7 * pieces + 7 :]
    if final:
        (raw_ref, rate_ref), refs = refs[:2], refs[2:]
    if prior:
        (sums_in, edge_in), refs = refs[:2], refs[4:]
    out_hbm, din_hbm, dquery_ref, dkey_ref, *results, out_ref, din_ref, sems = refs
    rows, state_size = dquery_in.shape
    firsts, _ = place()
    rise = sink = edge = dlead = dtail = None
    if prior:
        rise, sink, edge = sums_in[0], sums_in[1], edge_in[...]
    copies = []
    for i, block in enumerate(blocks):
        local_out_ref, local_din_ref, grown_ref, fallen_ref, grow_ref, fall_ref, sums_ref = block
        here = slice(i * tile, (i + 1) * tile)
        there = slice(first_column + i * tile, first_column + (i + 1) * tile)
        entering = inward(firsts, took_ref[0, :, here], own_ref[0, :, here])
        leaving = inward(firsts, took_ref[1, :, here], own_ref[1, :, here])
        grown = grown_ref[...]
        fallen = fallen_ref[...]
        entering_bf = entering.astype(BF16)
        leaving_bf = (leaving * rows_ref[1:2, there]).astype(BF16)
        reached = dot_nn(maps_ref[:, :state_size], entering_bf)
        behind = dot_nn(maps_ref[:, state_size:], leaving_bf)
        out_ref[:, here] = (local_out_ref[...] + fall_ref[...].astype(F32) * reached).astype(BF16)
        din_ref[:, here] = (local_din_ref[...] + grow_ref[...].astype(F32) * behind).astype(BF16)
        for j, (source, target) in enumerate(((out_ref, out_hbm), (din_ref, din_hbm))):
            copy = pltpu.make_async_copy(
                source.at[:, pl.ds(here.start, tile)], target.at[:, pl.ds(there.start, tile)],
                sems.at[2 * i + j],
            )
            copy.start()
            copies.append(copy)
        collect = head_collect(head_count, there.start, tile, head_size)
        rise_now = dot_nn((fallen.astype(F32) * reached).astype(BF16), collect) + sums_ref[0]
        pulled = grown.astype(F32) * behind
        sink_now = dot_nn(pulled.astype(BF16), collect) + sums_ref[1]
        edge_row = jnp.sum(pulled, axis=0, keepdims=True) + rows_ref[0:1, there] * jnp.sum(
            entering * leaving, axis=0, keepdims=True
        )
        high, rest = halves(jnp.broadcast_to(edge_row, (8, tile)))
        edge_now = dot_nn(high, collect) + dot_nn(rest, collect)
        dlead_now = dot_nt(fallen, entering_bf)
        dtail_now = dot_nt(grown, leaving_bf)
        rise = rise_now if rise is None else rise + rise_now
        sink = sink_now if sink is None else sink + sink_now
        edge = edge_now if edge is None else edge + edge_now
        dlead = dlead_now if dlead is None else dlead + dlead_now
        dtail = dtail_now if dtail is None else dtail + dtail_now
    in_lead = heads_ref[:, 4 * head_count : 4 * head_count + 1].astype(F32) > 0.5
    in_tail = heads_ref[:, 4 * head_count + 1 : 4 * head_count + 2].astype(F32) > 0.5
    dquery_ref[...] = (dquery_in[...] + jnp.where(in_lead, dlead, 0.0)).astype(dquery_ref.dtype)
    dkey_ref[...] = (dkey_in[...] + jnp.where(in_tail, dtail, 0.0)).astype(dkey_ref.dtype)
    if final:
        lower = triangle(rows, True).astype(F32).astype(BF16)
        sink_turned = sink.T
        later = sum_dot_left(rise.T - sink_turned, lower) + edge.T[:, :1]
        raw = raw_ref[...]
        rate = jnp.broadcast_to(rate_ref[...], (8, head_count)).T[:, :1]
        results[0][...] = (sink_turned / softplus(raw) - rate * later) / (1.0 + jnp.exp(-raw))
    else:
        results[0][0] = rise
        results[0][1] = sink
        results[1][...] = edge
    for copy in copies:
        copy.wait()


def schedule(widths, tiles, levels):
    total = sum(widths)
    chunks = len(widths)
    pieces = [tile for width, tile in zip(widths, tiles) for _ in range(width // tile)]
    middle = ["climb"] * (levels - 1)
    stages = ["chip", "plane", "pair"] + middle + ["top", "side", "device", "end"]
    moves = [15.6, 7.8] + [5.8] * levels + [7.8, 15.6, 3.0, 0.0]
    links = ["side", "low"] + ["high"] * levels + ["low", "side", "core", None]
    at = [0] * chunks
    ready = [3.0 + 0.3 * k for k in range(chunks)]
    free = {}
    now, blocks, order, ended = 3.0, 0, [], 0
    while ended < chunks:
        chain = [k for k in range(chunks) if at[k] < len(stages) - 1]
        soon = min(chain, key=lambda k: (ready[k], -at[k]), default=None)
        work = 11.0 * widths[ended] / total
        left = blocks < len(pieces)
        block = 11.5 * pieces[blocks] / total if left else 0.0
        can_end = at[ended] == len(stages) - 1 and not left
        fits = soon is not None and now + block <= ready[soon] + SLACK
        if left and min(at) > 0 and (fits or soon is None):
            order.append(("parts", blocks))
            now += block
            blocks += 1
            continue
        if soon is None:
            pick = ended
        elif can_end and max(now, ready[ended]) + work <= ready[soon] + 3.0:
            pick = ended
        else:
            pick = soon
        now = max(now, ready[pick])
        stage = stages[at[pick]]
        order.append((stage, pick))
        if stage == "end":
            now += work
            ended += 1
            at[pick] += 1
            continue
        now += 1.6
        link = links[at[pick]]
        begin = max(now, free.get(link, 0.0))
        free[link] = begin + moves[at[pick]] * widths[pick] / total
        ready[pick] = free[link] + 0.5
        at[pick] += 1
    return order


def params():
    return pltpu.CompilerParams(vmem_limit_bytes=VMEM_BYTES)


def cost(flops, count):
    return pl.CostEstimate(flops=flops, bytes_accessed=count, transcendentals=0)


def after(kernel, count, extra):
    def run(*refs):
        kernel(*refs[:count], *refs[count + extra :])

    return run


ANY = pl.BlockSpec(memory_space=pl.ANY)
HBM = pl.BlockSpec(memory_space=pltpu.HBM)
NEAR = pl.BlockSpec(memory_space=pltpu.VMEM)


def local(inputs, raw_steps, input_map, output_map, decay_rates, skip_gain, starts, cotangent):
    rows, channels = inputs.shape
    head_count = decay_rates.shape[0]
    head_size = channels // head_count
    state_size = input_map.shape[1]
    eighth = state_size // 8
    unit = channels // sum(WIDTHS)
    widths = [count * unit for count in WIDTHS]
    tile_of = [count * unit for count in TILES]
    chunks = len(widths)
    firsts = [sum(widths[:k]) for k in range(chunks)]

    size = lax.axis_size("seq")
    planes = size // 8
    levels = planes.bit_length() - 1
    starts_row = starts.reshape(1, rows)
    rate_row = decay_rates.reshape(1, head_count)
    skip_heads = skip_gain.reshape(1, head_count)
    raw_turned = raw_steps.T

    def far(value):
        return pltpu.with_memory_space_constraint(value, pltpu.HBM)

    def shape(dims, kind=F32):
        return jax.ShapeDtypeStruct(dims, kind)

    heads, maps, turned, wide_rows, decay = pl.pallas_call(
        functools.partial(prep_kernel, head_size),
        out_shape=(
            shape((rows, 4 * head_count + 2), BF16),
            shape((rows, 2 * state_size), BF16),
            shape((2 * state_size, rows), BF16),
            shape((8, channels)),
            shape((1, channels)),
        ),
        in_specs=[HBM] * 6,
        scratch_shapes=[
            pltpu.VMEM((head_count, rows), F32), pltpu.VMEM((1, head_count), F32),
            pltpu.VMEM((1, head_count), F32), pltpu.VMEM((1, rows), jnp.int32),
            pltpu.VMEM((rows, state_size), BF16), pltpu.VMEM((rows, state_size), BF16),
            pltpu.SemaphoreType.DMA((6,)),
        ],
        compiler_params=params(),
        name="prep",
    )(*(far(v) for v in (raw_turned, rate_row, skip_heads, starts_row, output_map, input_map)))

    row_shape = shape((1, channels))

    def flat_shape(chunk):
        return shape((eighth, widths[chunk]))

    def pair_shape(chunk, scale=1):
        return shape((2, scale * eighth, widths[chunk]))

    def tile_scratch(chunk):
        block = (rows, widths[chunk])
        return [
            pltpu.VMEM(block, BF16), pltpu.VMEM(block, BF16),
            pltpu.SemaphoreType.DMA((2 * widths[chunk] // tile_of[chunk],)),
        ]

    def device_states(chunk, last):
        kernel = functools.partial(
            states_kernel, head_count, head_size, firsts[chunk], tile_of[chunk]
        )
        return pl.pallas_call(
            after(kernel, 5, len(last)),
            out_shape=(pair_shape(chunk, 4), pair_shape(chunk, 4)),
            in_specs=[HBM, HBM, NEAR, NEAR, NEAR] + [ANY] * len(last),
            scratch_shapes=tile_scratch(chunk),
            compiler_params=params(),
            cost_estimate=cost(STATES_COST, 1000),
            name="states",
        )(far(inputs), far(cotangent), heads, turned, wide_rows, *last)

    def swap(value, bit):
        return lax.ppermute(value, "seq", [(i, i ^ bit) for i in range(size)])

    def level_perms(level):
        span = 1 << level
        perms = []
        for shift in range(span):
            pairs = []
            for base in range(0, planes, 2 * span):
                pairs.append((base + span - 1, base + span + shift))
                pairs.append((base + span, base + span - 1 - shift))
            perms.append([(8 * a + r, 8 * b + r) for a, b in pairs for r in range(8)])
        return perms

    held = {"last": ()}

    def small(kernel, out_shape, name, *operands):
        last = held["last"]
        return pl.pallas_call(
            after(kernel, len(operands), len(last)),
            out_shape=out_shape,
            in_specs=[NEAR] * len(operands) + [ANY] * len(last),
            compiler_params=params(),
            cost_estimate=cost(SMALL_COST, 1000),
            name=name,
        )(*operands, *last)

    tiles = [
        (k, firsts[k] + i * tile_of[k], tile_of[k])
        for k in range(chunks)
        for i in range(widths[k] // tile_of[k])
    ]

    def block_parts(piece, sofar):
        last = held["last"]
        initial = piece == 0
        final = piece == len(tiles) - 1
        _, first, tile = tiles[piece]
        square = (rows, rows)
        block = (rows, tile)
        outs = [shape(block)] * 2 + [shape(block, BF16)] * 4 + [shape((2, rows, head_count))]
        if initial:
            outs += [shape(square, BF16), shape(square, BF16)]
        outs += [shape((rows, state_size))] * 2 if final else [shape(square)]
        operands = [
            far(inputs), far(cotangent), heads, wide_rows, starts_row, output_map, input_map,
        ] + list(sofar)
        kernel = functools.partial(local_kernel, head_count, head_size, first, initial, final)
        made = pl.pallas_call(
            after(kernel, len(operands), len(last)),
            out_shape=tuple(outs),
            in_specs=[HBM, HBM] + [NEAR] * (len(operands) - 2) + [ANY] * len(last),
            scratch_shapes=[
                pltpu.VMEM(block, BF16), pltpu.VMEM(block, BF16), pltpu.SemaphoreType.DMA((2,)),
            ],
            compiler_params=params(),
            cost_estimate=cost(1000, 1000),
            name="block",
        )(*operands, *last)
        if final:
            return made[:7], tuple(made[-2:])
        if initial:
            return made[:7], tuple(made[7:])
        return made[:7], (sofar[0], sofar[1], made[7])

    def finish(chunk, blocks, took, own, grads, prior):
        flat = (rows, state_size)
        tile = tile_of[chunk]
        last = held["last"]
        final = chunk == chunks - 1
        operands = [value for block in blocks for value in block]
        operands += [took, own, wide_rows, heads, maps, *grads]
        if final:
            operands += [raw_turned, rate_row]
        in_specs = [NEAR] * len(operands)
        aliases = {}
        if prior:
            aliases = {len(operands) + 2: 0, len(operands) + 3: 1}
            operands += list(prior)
            in_specs += [NEAR, NEAR, ANY, ANY]
        kind = BF16 if final else F32
        ends = [shape((head_count, rows))]
        if not final:
            ends = [shape((2, rows, head_count)), shape((8, head_count))]
        kernel = functools.partial(
            finish_kernel, head_count, head_size, firsts[chunk], tile, len(blocks), bool(prior),
            final,
        )
        result = shape((rows, widths[chunk]), BF16)
        return pl.pallas_call(
            after(kernel, len(operands), len(last)),
            out_shape=(
                shape((rows, channels), BF16), shape((rows, channels), BF16),
                shape(flat, kind), shape(flat, kind), *ends,
            ),
            in_specs=in_specs + [ANY] * len(last),
            out_specs=(ANY, ANY, NEAR, NEAR) + (NEAR,) * len(ends),
            scratch_shapes=[
                pltpu.VMEM(result.shape, BF16), pltpu.VMEM(result.shape, BF16),
                pltpu.SemaphoreType.DMA((2 * widths[chunk] // tile,)),
            ],
            input_output_aliases=aliases,
            compiler_params=params(),
            cost_estimate=cost(1000, 1000),
            name="finish",
        )(*operands, *last)

    every = range(chunks)
    span = [slice(firsts[k], firsts[k] + widths[k]) for k in every]

    def join(k, level):
        kept, came = held["kept", k, level]
        own_decay, other_decay = held["decay", level]
        sent = flat_shape(k) if level == 2 else pair_shape(k, 2 - level)
        made = (sent, pair_shape(k, max(1, 2 - level)))
        if level == 2 and levels == 1:
            made = made[:1]
        sent, *kept = small(
            functools.partial(join_kernel, span[k], level), made, "join",
            kept, came, own_decay, other_decay,
        )
        kept = kept[0] if kept else None
        held["last"] = (sent,)
        if level == 2:
            held["level", k] = (sent, kept, None, 0)
            send(k)
        else:
            held["kept", k, level + 1] = (kept, swap(sent, 2 << level))

    def parts(k):
        held["block", k], held["sofar"] = block_parts(k, held.get("sofar", ()))
        held["last"] = (held["block", k][6],)

    def taken(k, level):
        pay = held["level", k][0]
        return [lax.ppermute(pay, "seq", perm) for perm in level_perms(level)]

    def send(k):
        held["taken", k] = taken(k, held["level", k][3])

    def climb(k):
        _, both, enter, level = held["level", k]
        came = held["taken", k]
        operands = came + held["others"][:level] + ([enter] if level else [])
        pay, enter = small(
            functools.partial(level_kernel, span[k], level, len(came)),
            (flat_shape(k), pair_shape(k)), "level", *operands, both, held["unit"],
        )
        held["level", k] = (pay, both, enter, level + 1)
        held["last"] = (pay,)
        send(k)

    def top(k):
        kept, came = held["kept", k, 2]
        _, _, enter, level = held["level", k]
        got = held["taken", k]
        operands = got + held["others"][:level] + ([enter] if level else [])
        theirs, mine = small(
            functools.partial(top_kernel, span[k], level, len(got)),
            (pair_shape(k), pair_shape(k)), "top", *operands, kept, came,
            *held["decay", 2],
        )
        held["back", k, 2] = (mine, swap(theirs, 4))
        held["last"] = (theirs,)

    def give_back(k, level):
        mine, back = held["back", k, level + 1]
        kept, came = held["kept", k, level]
        made = pair_shape(k, 4 >> level)
        give, own = small(
            functools.partial(return_kernel, span[k], level), (made, made), "return",
            back, mine, kept, came, *held["decay", level],
        )
        held["back", k, level] = (own, swap(give, 1 << level))
        held["last"] = (give,)

    def end(k):
        own, took = held["back", k, 0]
        blocks = [held["block", i] for i, (owner, _, _) in enumerate(tiles) if owner == k]
        out, din, dquery, dkey, *sums = finish(
            k, blocks, took, own, held["sofar"], held.get("prior", ())
        )
        held["sofar"] = (dquery, dkey)
        held["prior"] = (*sums, out, din)
        held["last"] = (sums[0],)

    decay_other = swap(decay, 1)
    across = swap(decay, 2)
    corner = swap(decay, 3)
    held["decay", 0] = (decay, decay_other)
    chip_decay = decay * decay_other
    chip_other = across * corner
    held["decay", 1] = (chip_decay, chip_other)
    plane_decay = chip_decay * chip_other
    last = ()
    for k in every:
        sent, kept = device_states(k, last)
        held["kept", k, 0] = (kept, swap(sent, 1))
        last = (plane_decay, sent)
    held["last"] = (sent,)
    plane_other = swap(plane_decay, 4)
    held["decay", 2] = (plane_decay, plane_other)
    group = held["unit"] = plane_decay * plane_other
    others = held["others"] = []
    for level in range(levels - 1):
        other = swap(group, 8 << level)
        others.append(other)
        group = group * other

    for name, k in schedule(WIDTHS, TILES, levels):
        if name == "chip":
            join(k, 0)
        elif name == "parts":
            held["last"] += (plane_other,)
            parts(k)
        elif name == "plane":
            join(k, 1)
        elif name == "pair":
            join(k, 2)
        elif name == "climb":
            climb(k)
        elif name == "top":
            top(k)
        elif name == "side":
            give_back(k, 1)
        elif name == "device":
            give_back(k, 0)
        else:
            end(k)
    draw, out, din = held["prior"]
    dquery, dkey = held["sofar"]
    return out, din, draw.T, dkey, dquery


def solution(mesh):
    sequence = P(("groups", "seq"), None)
    return jax.shard_map(
        local,
        mesh=mesh,
        in_specs=(
            sequence, sequence, sequence, sequence, P(), P(), P(("groups", "seq")), sequence,
        ),
        out_specs=(sequence,) * 5,
        check_vma=False,
    )
```

```python
import functools

import jax
import jax.numpy as jnp
from jax import lax
from jax.experimental import pallas as pl
from jax.experimental.pallas import tpu as pltpu
from jax.sharding import PartitionSpec as P

WIDTHS = (10, 10)
TILES = (5, 5)
SMALL_COST = 1000
STATES_COST = 4_000_000_000
VMEM_BYTES = 28 * 1024 * 1024

F32 = jnp.float32
BF16 = jnp.bfloat16


def dot_nn(left, right):
    return lax.dot_general(left, right, (((1,), (0,)), ((), ())), preferred_element_type=F32)


def dot_nt(left, right):
    return lax.dot_general(left, right, (((1,), (1,)), ((), ())), preferred_element_type=F32)


def halves(value):
    high = value.astype(BF16)
    return high, (value - high.astype(F32)).astype(BF16)


def sum_dot(matrix, value):
    first = value.astype(BF16)
    rest = value - first.astype(F32)
    second = rest.astype(BF16)
    third = (rest - second.astype(F32)).astype(BF16)
    return dot_nn(matrix, first) + dot_nn(matrix, second) + dot_nn(matrix, third)


def head_spread(depth, offset, head_count, first_column, columns, head_size):
    row = lax.broadcasted_iota(jnp.int32, (depth, columns), 0) - offset
    held = (row >= 0) & (row < 2 * head_count)
    row = jnp.where(row >= head_count, row - head_count, row)
    column = lax.broadcasted_iota(jnp.int32, (depth, columns), 1) + first_column
    inside = column - row * head_size
    return jnp.where(held & (inside >= 0) & (inside < head_size), 1.0, 0.0).astype(BF16)


def head_collect(head_count, first_column, columns, head_size):
    row = lax.broadcasted_iota(jnp.int32, (columns, head_count), 0) + first_column
    column = lax.broadcasted_iota(jnp.int32, (columns, head_count), 1)
    offset = row - column * head_size
    return jnp.where((offset >= 0) & (offset < head_size), 1.0, 0.0).astype(BF16)


def triangle(rows, lower):
    first = lax.broadcasted_iota(jnp.int32, (rows, rows), 0)
    second = lax.broadcasted_iota(jnp.int32, (rows, rows), 1)
    return (first >= second) if lower else (first <= second)


def start_counts(starts_row):
    rows = starts_row.shape[1]
    flags = starts_row.astype(F32)
    column = jnp.sum(jnp.where(triangle(rows, True), flags, 0.0), axis=1, keepdims=True)
    spread = jnp.broadcast_to(flags, (8, rows)).astype(BF16)
    row = dot_nn(spread, triangle(rows, False).astype(F32).astype(BF16))[:1]
    return column, row


def softplus(value):
    return jnp.maximum(value, 0.0) + jnp.log1p(jnp.exp(-jnp.abs(value)))


def sum_dot_left(value, matrix):
    first = value.astype(BF16)
    rest = value - first.astype(F32)
    second = rest.astype(BF16)
    third = (rest - second.astype(F32)).astype(BF16)
    return dot_nn(first, matrix) + dot_nn(second, matrix) + dot_nn(third, matrix)


def fetch(pairs, sems):
    copies = [
        pltpu.make_async_copy(source, target, sems.at[i])
        for i, (source, target) in enumerate(pairs)
    ]
    for copy in copies:
        copy.start()
    return copies


def prep_kernel(
    head_size, raw_hbm, rate_hbm, skip_hbm, starts_hbm, query_hbm, key_hbm,
    heads_ref, maps_ref, turned_ref, rows_ref, decay_ref,
    raw_ref, rate_ref, skip_ref, starts_ref, query_ref, key_ref, sems,
):
    copies = fetch(
        [
            (raw_hbm, raw_ref), (rate_hbm, rate_ref), (skip_hbm, skip_ref),
            (starts_hbm, starts_ref), (query_hbm, query_ref), (key_hbm, key_ref),
        ],
        sems,
    )
    head_count, rows = raw_ref.shape
    upper = triangle(rows, False).astype(F32).astype(BF16)
    for copy in copies:
        copy.wait()
    step = softplus(raw_ref[...])
    rate = jnp.broadcast_to(rate_ref[...], (8, head_count)).T[:, :1]
    cumulative = sum_dot_left(-step * rate, upper)
    count, _ = start_counts(starts_ref[...])
    in_lead = count == 0.0
    in_tail = count == count[rows - 1 :, :]
    state_size = query_ref.shape[1]
    lead = jnp.where(in_lead, query_ref[...].astype(F32), 0.0)
    tail = jnp.where(in_tail, key_ref[...].astype(F32), 0.0)
    maps_ref[:, :state_size] = lead.astype(BF16)
    maps_ref[:, state_size:] = tail.astype(BF16)
    turned_ref[:state_size] = lead.T.astype(BF16)
    turned_ref[state_size:] = tail.T.astype(BF16)
    fall = jnp.exp(cumulative).T
    grow = (jnp.exp(-cumulative) * step).T
    heads_ref[...] = jnp.concatenate(
        halves(fall)
        + halves(grow)
        + (
            jnp.where(in_lead, 1.0, 0.0).astype(BF16),
            jnp.where(in_tail, 1.0, 0.0).astype(BF16),
        ),
        axis=1,
    )
    channels = rows_ref.shape[1]
    spread = head_spread(2 * head_count, 0, head_count, 0, channels, head_size)

    def wide(value):
        return dot_nn(
            jnp.concatenate(halves(jnp.broadcast_to(value, (8, head_count))), axis=1), spread
        )[:1]

    last = wide(fall[rows - 1 :, :])
    decay = jnp.where(count[rows - 1 :, :] == 0.0, last, 0.0)
    rows_ref[0:1, :] = decay
    rows_ref[1:2, :] = last
    rows_ref[2:3, :] = wide(skip_ref[...])
    decay_ref[...] = decay


def place():
    index = lax.axis_index("seq")
    return ((index & 1) == 0, (index & 2) == 0, (index & 4) == 0), index >> 3


def outward(firsts, value):
    half = value.shape[0] // 2
    low, high = value[:half], value[half:]
    other, own = jnp.where(firsts[0], high, low), jnp.where(firsts[0], low, high)
    if len(firsts) > 1:
        other, own = outward(firsts[1:], other), outward(firsts[1:], own)
    return jnp.concatenate([other, own], axis=0)


def inward(firsts, other, own):
    if len(firsts) > 1:
        half = own.shape[0] // 2
        other = inward(firsts[1:], other[:half], other[half:])
        own = inward(firsts[1:], own[:half], own[half:])
    low, high = jnp.where(firsts[0], own, other), jnp.where(firsts[0], other, own)
    return jnp.concatenate([low, high], axis=0)


def joined(first, own_decay, other_decay, own, came):
    one = jnp.ones_like(own_decay)
    forward = (
        jnp.where(first, other_decay, one) * own[0] + jnp.where(first, one, own_decay) * came[0]
    )
    backward = (
        jnp.where(first, one, other_decay) * own[1] + jnp.where(first, own_decay, one) * came[1]
    )
    return forward, backward


def split_pair(first, own_decay, other_decay, own, came, entering, leaving, put_own, put_other):
    @pl.when(first)
    def _():
        put_own(0, entering)
        put_other(0, own_decay * entering + own(0))
        put_other(1, leaving)
        put_own(1, other_decay * leaving + came(1))

    @pl.when(jnp.logical_not(first))
    def _():
        put_other(0, entering)
        put_own(0, other_decay * entering + came(0))
        put_own(1, leaving)
        put_other(1, own_decay * leaving + own(1))


def join_kernel(columns, kept_ref, came_ref, own_ref, other_ref, *results):
    firsts, _ = place()
    forward, backward = joined(
        firsts[0], own_ref[:, columns], other_ref[:, columns], kept_ref, came_ref
    )
    quarter = forward.shape[0] // 4
    for slot, ref in enumerate(results):
        here = slice(slot * quarter, (slot + 1) * quarter)
        ref[:quarter] = forward[here]
        ref[quarter : 2 * quarter] = backward[here]
        if ref.shape[0] > 2 * quarter:
            width = ref.shape[1]
            for chunk in range(own_ref.shape[1] // width):
                there = slice(chunk * width, (chunk + 1) * width)
                row = 2 * quarter + chunk
                ref[row : row + 1, :] = own_ref[:, there] * other_ref[:, there]


def four_chips(firsts, row, values, decays):
    half = decays[0].shape[0] - 8
    quarter = half // 2
    return (
        in_order(firsts, *(ref[half + row : half + row + 1, :] for ref in decays)),
        in_order(firsts, *(ref[:quarter] for ref in values)),
        in_order(firsts, *(ref[quarter:half] for ref in values)),
    )


def in_order(firsts, own, side, depth, corner):
    _, near, low = firsts
    first, second = jnp.where(near, own, side), jnp.where(near, side, own)
    third, fourth = jnp.where(near, depth, corner), jnp.where(near, corner, depth)
    return (
        jnp.where(low, first, third), jnp.where(low, second, fourth),
        jnp.where(low, third, first), jnp.where(low, fourth, second),
    )


def for_chips(firsts, values):
    _, near, low = firsts
    first, second = jnp.where(low, values[0], values[2]), jnp.where(low, values[1], values[3])
    third, fourth = jnp.where(low, values[2], values[0]), jnp.where(low, values[3], values[1])
    return (
        jnp.where(near, first, second), jnp.where(near, second, first),
        jnp.where(near, third, fourth), jnp.where(near, fourth, third),
    )


def quad_kernel(row, *refs):
    values, decays, results = refs[:4], refs[4:8], refs[8:]
    firsts, unit = place()
    decay, states, directs = four_chips(firsts, row, values, decays)
    forward, backward = states[0], directs[3]
    for i in (1, 2, 3):
        forward = decay[i] * forward + states[i]
        backward = directs[3 - i] + decay[3 - i] * backward
    results[0][...] = jnp.where((unit & 1) == 1, backward, forward)
    if len(results) > 1:
        results[1][0] = forward
        results[1][1] = backward


def absorb(columns, level, plane, taken_refs, others, enter_ref):
    upper = ((plane >> level) & 1) == 1
    taken = taken_refs[0][...]
    for ref in taken_refs[1:]:
        taken = taken + ref[...]
    if level == 0:
        zero = jnp.zeros_like(taken)
        return jnp.where(upper, taken, zero), jnp.where(upper, zero, taken)
    before = after = None
    for lower, ref in enumerate(others[:level]):
        other = ref[:, columns]
        above = ((plane >> lower) & 1) == 1
        one = jnp.ones_like(other)
        first = jnp.where(above, other, one)
        second = jnp.where(above, one, other)
        before = first if before is None else before * first
        after = second if after is None else after * second
    zero = jnp.zeros_like(before)
    return (
        enter_ref[0] + jnp.where(upper, before, zero) * taken,
        enter_ref[1] + jnp.where(upper, zero, after) * taken,
    )


def level_kernel(columns, level, taken_count, *refs):
    taken, refs = refs[:taken_count], refs[taken_count:]
    others, refs = refs[:level], refs[level:]
    enter_ref = None
    if level:
        enter_ref, refs = refs[0], refs[1:]
    both_ref, decay_ref, pay_ref, next_ref = refs
    _, plane = place()
    entering, leaving = absorb(columns, level, plane, taken, others, enter_ref)
    next_ref[0] = entering
    next_ref[1] = leaving
    upper = ((plane >> (level + 1)) & 1) == 1
    decay = decay_ref[:, columns]

    @pl.when(upper)
    def _():
        pay_ref[...] = decay * leaving + both_ref[1]

    @pl.when(jnp.logical_not(upper))
    def _():
        pay_ref[...] = decay * entering + both_ref[0]


def top_kernel(columns, row, level, taken_count, *refs):
    taken, refs = refs[:taken_count], refs[taken_count:]
    others, refs = refs[:level], refs[level:]
    enter_ref = None
    if level:
        enter_ref, refs = refs[0], refs[1:]
    values, decays, results = refs[:4], refs[4:8], refs[8:]
    firsts, unit = place()
    entering, leaving = absorb(columns, level, unit, taken, others, enter_ref)
    decay, states, directs = four_chips(firsts, row, values, decays)
    enters, leaves = [entering], [leaving]
    for i in (0, 1, 2):
        enters.append(decay[i] * enters[-1] + states[i])
        leaves.append(decay[3 - i] * leaves[-1] + directs[3 - i])
    for chain, value in enumerate((enters, leaves[::-1])):
        for ref, part in zip(results, for_chips(firsts, value)):
            ref[chain] = part


def return_kernel(columns, *refs):
    sources = refs[:4]
    kept_ref, came_ref, own_ref, other_ref, give_ref, stay_ref = refs[4:]
    first = place()[0][0]
    quarter = sources[0].shape[1]
    for slot, source in enumerate(sources):
        here = slice(slot * quarter, (slot + 1) * quarter)

        def put_own(chain, value, here=here):
            stay_ref[chain, here] = value

        def put_other(chain, value, here=here):
            give_ref[chain, here] = value

        split_pair(
            first, own_ref[:, columns], other_ref[:, columns],
            lambda i, here=here: kept_ref[i, here], lambda i, here=here: came_ref[i, here],
            source[0], source[1], put_own, put_other,
        )


def scale_columns(heads_ref, head_count, head_size, first, columns):
    heads = heads_ref[...]
    depth = heads.shape[1]
    args = (head_count, first, columns, head_size)
    fall = dot_nn(heads, head_spread(depth, 0, *args))
    grow = dot_nn(heads, head_spread(depth, 2 * head_count, *args))
    return fall, grow


def load_tiles(in_hbm, cot_hbm, in_ref, cot_ref, sems, first, tile):
    found = []
    for i in range(in_ref.shape[1] // tile):
        here = pl.ds(first + i * tile, tile)
        there = pl.ds(i * tile, tile)
        pair = []
        for j, (source, target) in enumerate(((in_hbm, in_ref), (cot_hbm, cot_ref))):
            copy = pltpu.make_async_copy(
                source.at[:, here], target.at[:, there], sems.at[2 * i + j]
            )
            copy.start()
            pair.append(copy)
        found.append(pair)
    return found


def states_kernel(
    head_count, head_size, first_column, tile, in_hbm, cot_hbm, heads_ref, turned_ref, rows_ref,
    send_ref, keep_ref, in_ref, cot_ref, sems,
):
    copies = load_tiles(in_hbm, cot_hbm, in_ref, cot_ref, sems, first_column, tile)
    firsts, _ = place()
    state_size = turned_ref.shape[0] // 2
    for i, pair in enumerate(copies):
        here = slice(i * tile, (i + 1) * tile)
        there = slice(first_column + i * tile, first_column + (i + 1) * tile)
        fall, grow = scale_columns(heads_ref, head_count, head_size, there.start, tile)
        for copy in pair:
            copy.wait()
        grown = (grow * in_ref[:, here].astype(F32)).astype(BF16)
        fallen = (fall * cot_ref[:, here].astype(F32)).astype(BF16)
        state = dot_nn(turned_ref[state_size:], grown) * rows_ref[1:2, there]
        direct = dot_nn(turned_ref[:state_size], fallen)
        half = state_size // 2
        for chain, value in enumerate((state, direct)):
            value = outward(firsts, value)
            send_ref[chain, :, here] = value[:half]
            keep_ref[chain, :, here] = value[half:]


def local_kernel(
    head_count, head_size, first_column, initial, final, in_hbm, cot_hbm, heads_ref, rows_ref,
    starts_ref, query_ref, key_ref, *refs,
):
    if not initial:
        score_ref, scoret_ref, total_in, refs = *refs[:3], refs[3:]
    out_ref, din_ref, grown_ref, fallen_ref, grow_ref, fall_ref, sums_ref = refs[:7]
    refs = refs[7:]
    if initial:
        (score_ref, scoret_ref), refs = refs[:2], refs[2:]
    (total_out, *key_out), (in_ref, cot_ref, sems) = refs[:-3], refs[-3:]
    rows, columns = in_ref.shape
    ((in_copy, cot_copy),) = load_tiles(
        in_hbm, cot_hbm, in_ref, cot_ref, sems, first_column, columns
    )
    if initial or final:
        column, row = start_counts(starts_ref[...])
        same = column == row
        allowed = same & triangle(rows, True)
    if initial:
        score_ref[...] = jnp.where(allowed, dot_nt(query_ref[...], key_ref[...]), 0.0).astype(BF16)
        scoret_ref[...] = jnp.where(
            same & triangle(rows, False), dot_nt(key_ref[...], query_ref[...]), 0.0
        ).astype(BF16)
    fall, grow = scale_columns(heads_ref, head_count, head_size, first_column, columns)
    fall_ref[...] = fall.astype(BF16)
    grow_ref[...] = grow.astype(BF16)
    collect = head_collect(head_count, first_column, columns, head_size)
    in_copy.wait()
    cot_copy.wait()
    in_wide = in_ref[...].astype(F32)
    cot_wide = cot_ref[...].astype(F32)
    skip = rows_ref[2:3, first_column : first_column + columns]
    grown = (grow * in_wide).astype(BF16)
    fallen = (fall * cot_wide).astype(BF16)
    grown_ref[...] = grown
    fallen_ref[...] = fallen
    total = dot_nt(fallen, grown)
    if not initial:
        total += total_in[...]
    produced = dot_nn(score_ref[...], grown)
    out_ref[...] = fall * produced + skip * in_wide
    sums_ref[0] = dot_nn((fallen.astype(F32) * produced).astype(BF16), collect)
    pulled = dot_nn(scoret_ref[...], fallen)
    din_ref[...] = grow * pulled + skip * cot_wide
    sums_ref[1] = dot_nn((grown.astype(F32) * pulled).astype(BF16), collect)
    if final:
        grads = jnp.where(allowed, total, 0.0)
        total_out[...] = dot_nn(grads.astype(BF16), key_ref[...])
        key_out[0][...] = dot_nn(grads.T.astype(BF16), query_ref[...])
    else:
        total_out[...] = total


def finish_kernel(
    head_count, head_size, first_column, tile, pieces, prior, final, *refs,
):
    blocks = [refs[7 * i : 7 * i + 7] for i in range(pieces)]
    (took_ref, own_ref, rows_ref, heads_ref, maps_ref) = refs[7 * pieces : 7 * pieces + 5]
    refs = refs[7 * pieces + 5 :]
    if final:
        (dquery_in, dkey_in, raw_ref, rate_ref), refs = refs[:4], refs[4:]
    if prior:
        (sums_in, edge_in, dlead_in, dtail_in), refs = refs[:4], refs[6:]
    out_hbm, din_hbm, dquery_ref, dkey_ref, *results, out_ref, din_ref, sems = refs
    state_size = maps_ref.shape[1] // 2
    rows = heads_ref.shape[0]
    firsts, _ = place()
    rise = sink = edge = dlead = dtail = None
    if prior:
        rise, sink, edge = sums_in[0], sums_in[1], edge_in[...]
        dlead, dtail = dlead_in[...], dtail_in[...]
    copies = []
    for i, block in enumerate(blocks):
        local_out_ref, local_din_ref, grown_ref, fallen_ref, grow_ref, fall_ref, sums_ref = block
        here = slice(i * tile, (i + 1) * tile)
        there = slice(first_column + i * tile, first_column + (i + 1) * tile)
        entering = inward(firsts, took_ref[0, :, here], own_ref[0, :, here])
        leaving = inward(firsts, took_ref[1, :, here], own_ref[1, :, here])
        grown = grown_ref[...]
        fallen = fallen_ref[...]
        entering_bf = entering.astype(BF16)
        leaving_bf = (leaving * rows_ref[1:2, there]).astype(BF16)
        reached = dot_nn(maps_ref[:, :state_size], entering_bf)
        behind = dot_nn(maps_ref[:, state_size:], leaving_bf)
        out_ref[:, here] = (local_out_ref[...] + fall_ref[...].astype(F32) * reached).astype(BF16)
        din_ref[:, here] = (local_din_ref[...] + grow_ref[...].astype(F32) * behind).astype(BF16)
        for j, (source, target) in enumerate(((out_ref, out_hbm), (din_ref, din_hbm))):
            copy = pltpu.make_async_copy(
                source.at[:, pl.ds(here.start, tile)], target.at[:, pl.ds(there.start, tile)],
                sems.at[2 * i + j],
            )
            copy.start()
            copies.append(copy)
        collect = head_collect(head_count, there.start, tile, head_size)
        rise_now = dot_nn((fallen.astype(F32) * reached).astype(BF16), collect) + sums_ref[0]
        pulled = grown.astype(F32) * behind
        sink_now = dot_nn(pulled.astype(BF16), collect) + sums_ref[1]
        edge_row = jnp.sum(pulled, axis=0, keepdims=True) + rows_ref[0:1, there] * jnp.sum(
            entering * leaving, axis=0, keepdims=True
        )
        high, rest = halves(jnp.broadcast_to(edge_row, (8, tile)))
        edge_now = dot_nn(high, collect) + dot_nn(rest, collect)
        dlead_now = dot_nt(fallen, entering_bf)
        dtail_now = dot_nt(grown, leaving_bf)
        rise = rise_now if rise is None else rise + rise_now
        sink = sink_now if sink is None else sink + sink_now
        edge = edge_now if edge is None else edge + edge_now
        dlead = dlead_now if dlead is None else dlead + dlead_now
        dtail = dtail_now if dtail is None else dtail + dtail_now
    if final:
        in_lead = heads_ref[:, 4 * head_count : 4 * head_count + 1].astype(F32) > 0.5
        in_tail = heads_ref[:, 4 * head_count + 1 : 4 * head_count + 2].astype(F32) > 0.5
        dquery_ref[...] = (dquery_in[...] + jnp.where(in_lead, dlead, 0.0)).astype(BF16)
        dkey_ref[...] = (dkey_in[...] + jnp.where(in_tail, dtail, 0.0)).astype(BF16)
        lower = triangle(rows, True).astype(F32).astype(BF16)
        sink_turned = sink.T
        later = sum_dot_left(rise.T - sink_turned, lower) + edge.T[:, :1]
        raw = raw_ref[...]
        rate = jnp.broadcast_to(rate_ref[...], (8, head_count)).T[:, :1]
        results[0][...] = (sink_turned / softplus(raw) - rate * later) / (1.0 + jnp.exp(-raw))
    else:
        dquery_ref[...] = dlead
        dkey_ref[...] = dtail
        results[0][0] = rise
        results[0][1] = sink
        results[1][...] = edge
    for copy in copies:
        copy.wait()


def schedule(levels):
    climbs = [("climb", k) for _ in range(levels - 1) for k in (0, 1)]
    middle = [("top", 0), ("quad", 1)]
    if climbs:
        middle = [("quad", 1), *climbs, ("top", 0)]
    return [
        ("join", 0), ("parts", 0), ("join", 1), ("quad", 0), ("parts", 1), *middle, ("parts", 2),
        ("top", 1), ("device", 0), ("end", 0), ("parts", 3), ("device", 1), ("end", 1),
    ]


def params():
    return pltpu.CompilerParams(vmem_limit_bytes=VMEM_BYTES)


def cost(flops, count):
    return pl.CostEstimate(flops=flops, bytes_accessed=count, transcendentals=0)


def after(kernel, count, extra):
    def run(*refs):
        kernel(*refs[:count], *refs[count + extra :])

    return run


ANY = pl.BlockSpec(memory_space=pl.ANY)
HBM = pl.BlockSpec(memory_space=pltpu.HBM)
NEAR = pl.BlockSpec(memory_space=pltpu.VMEM)


def local(inputs, raw_steps, input_map, output_map, decay_rates, skip_gain, starts, cotangent):
    rows, channels = inputs.shape
    head_count = decay_rates.shape[0]
    head_size = channels // head_count
    state_size = input_map.shape[1]
    eighth = state_size // 8
    unit = channels // sum(WIDTHS)
    widths = [count * unit for count in WIDTHS]
    tile_of = [count * unit for count in TILES]
    chunks = len(widths)
    firsts = [sum(widths[:k]) for k in range(chunks)]

    size = lax.axis_size("seq")
    planes = size // 8
    levels = planes.bit_length() - 1
    starts_row = starts.reshape(1, rows)
    rate_row = decay_rates.reshape(1, head_count)
    skip_heads = skip_gain.reshape(1, head_count)
    raw_turned = raw_steps.T

    def far(value):
        return pltpu.with_memory_space_constraint(value, pltpu.HBM)

    def shape(dims, kind=F32):
        return jax.ShapeDtypeStruct(dims, kind)

    heads, maps, turned, wide_rows, decay = pl.pallas_call(
        functools.partial(prep_kernel, head_size),
        out_shape=(
            shape((rows, 4 * head_count + 2), BF16),
            shape((rows, 2 * state_size), BF16),
            shape((2 * state_size, rows), BF16),
            shape((8, channels)),
            shape((1, channels)),
        ),
        in_specs=[HBM] * 6,
        scratch_shapes=[
            pltpu.VMEM((head_count, rows), F32), pltpu.VMEM((1, head_count), F32),
            pltpu.VMEM((1, head_count), F32), pltpu.VMEM((1, rows), jnp.int32),
            pltpu.VMEM((rows, state_size), BF16), pltpu.VMEM((rows, state_size), BF16),
            pltpu.SemaphoreType.DMA((6,)),
        ],
        compiler_params=params(),
        name="prep",
    )(*(far(v) for v in (raw_turned, rate_row, skip_heads, starts_row, output_map, input_map)))

    row_shape = shape((1, channels))

    def flat_shape(chunk):
        return shape((eighth, widths[chunk]))

    def pair_shape(chunk, scale=1):
        return shape((2, scale * eighth, widths[chunk]))

    def tile_scratch(chunk):
        block = (rows, widths[chunk])
        return [
            pltpu.VMEM(block, BF16), pltpu.VMEM(block, BF16),
            pltpu.SemaphoreType.DMA((2 * widths[chunk] // tile_of[chunk],)),
        ]

    def device_states(chunk, last):
        kernel = functools.partial(
            states_kernel, head_count, head_size, firsts[chunk], tile_of[chunk]
        )
        return pl.pallas_call(
            after(kernel, 5, len(last)),
            out_shape=(pair_shape(chunk, 4), pair_shape(chunk, 4)),
            in_specs=[HBM, HBM, NEAR, NEAR, NEAR] + [ANY] * len(last),
            scratch_shapes=tile_scratch(chunk),
            compiler_params=params(),
            cost_estimate=cost(STATES_COST, 1000),
            name="states",
        )(far(inputs), far(cotangent), heads, turned, wide_rows, *last)

    def swap(value, bit):
        return lax.ppermute(value, "seq", [(i, i ^ bit) for i in range(size)])

    def level_perms(level):
        span = 1 << level
        perms = []
        for shift in range(span):
            pairs = []
            for base in range(0, planes, 2 * span):
                pairs.append((base + span - 1, base + span + shift))
                pairs.append((base + span, base + span - 1 - shift))
            perms.append([(8 * a + r, 8 * b + r) for a, b in pairs for r in range(8)])
        return perms

    held = {"last": ()}

    def small(kernel, out_shape, name, *operands):
        last = held["last"]
        return pl.pallas_call(
            after(kernel, len(operands), len(last)),
            out_shape=out_shape,
            in_specs=[NEAR] * len(operands) + [ANY] * len(last),
            compiler_params=params(),
            cost_estimate=cost(SMALL_COST, 1000),
            name=name,
        )(*operands, *last)

    tiles = [
        (k, firsts[k] + i * tile_of[k], tile_of[k])
        for k in range(chunks)
        for i in range(widths[k] // tile_of[k])
    ]

    def block_parts(piece, sofar):
        last = held["last"]
        initial = piece == 0
        final = piece == len(tiles) - 1
        _, first, tile = tiles[piece]
        square = (rows, rows)
        block = (rows, tile)
        outs = [shape(block)] * 2 + [shape(block, BF16)] * 4 + [shape((2, rows, head_count))]
        if initial:
            outs += [shape(square, BF16), shape(square, BF16)]
        outs += [shape((rows, state_size))] * 2 if final else [shape(square)]
        operands = [
            far(inputs), far(cotangent), heads, wide_rows, starts_row, output_map, input_map,
        ] + list(sofar)
        kernel = functools.partial(local_kernel, head_count, head_size, first, initial, final)
        made = pl.pallas_call(
            after(kernel, len(operands), len(last)),
            out_shape=tuple(outs),
            in_specs=[HBM, HBM] + [NEAR] * (len(operands) - 2) + [ANY] * len(last),
            scratch_shapes=[
                pltpu.VMEM(block, BF16), pltpu.VMEM(block, BF16), pltpu.SemaphoreType.DMA((2,)),
            ],
            compiler_params=params(),
            cost_estimate=cost(1000, 1000),
            name="block",
        )(*operands, *last)
        if final:
            return made[:7], tuple(made[-2:])
        if initial:
            return made[:7], tuple(made[7:])
        return made[:7], (sofar[0], sofar[1], made[7])

    def finish(chunk, blocks, took, own, grads, prior):
        flat = (rows, state_size)
        tile = tile_of[chunk]
        last = held["last"]
        final = chunk == chunks - 1
        operands = [value for block in blocks for value in block]
        operands += [took, own, wide_rows, heads, maps]
        if final:
            operands += [*grads, raw_turned, rate_row]
        in_specs = [NEAR] * len(operands)
        aliases = {}
        if prior:
            aliases = {len(operands) + 4: 0, len(operands) + 5: 1}
            operands += list(prior)
            in_specs += [NEAR] * 4 + [ANY, ANY]
        kind = BF16 if final else F32
        ends = [shape((head_count, rows))]
        if not final:
            ends = [shape((2, rows, head_count)), shape((8, head_count))]
        kernel = functools.partial(
            finish_kernel, head_count, head_size, firsts[chunk], tile, len(blocks), bool(prior),
            final,
        )
        result = shape((rows, widths[chunk]), BF16)
        return pl.pallas_call(
            after(kernel, len(operands), len(last)),
            out_shape=(
                shape((rows, channels), BF16), shape((rows, channels), BF16),
                shape(flat, kind), shape(flat, kind), *ends,
            ),
            in_specs=in_specs + [ANY] * len(last),
            out_specs=(ANY, ANY, NEAR, NEAR) + (NEAR,) * len(ends),
            scratch_shapes=[
                pltpu.VMEM(result.shape, BF16), pltpu.VMEM(result.shape, BF16),
                pltpu.SemaphoreType.DMA((2 * widths[chunk] // tile,)),
            ],
            input_output_aliases=aliases,
            compiler_params=params(),
            cost_estimate=cost(1000, 1000),
            name="finish",
        )(*operands, *last)

    every = range(chunks)
    span = [slice(firsts[k], firsts[k] + widths[k]) for k in every]

    def join(k):
        kept, came = held["kept", k]
        part = shape((2 * eighth + (8 if k == 0 else 0), widths[k]))
        corner, side, depth, stay = small(
            functools.partial(join_kernel, span[k]), (part,) * 4, "join",
            kept, came, decay, decay_other,
        )
        held["last"] = (side,)
        held["four", k] = (stay, swap(side, 2), swap(depth, 4), swap(corner, 6))

    def quad(k):
        made = (flat_shape(k),) + ((pair_shape(k),) if levels > 1 else ())
        pay, *both = small(
            functools.partial(quad_kernel, k), made, "quad", *held["four", k], *held["four", 0],
        )
        held["last"] = (pay,)
        held["level", k] = (pay, both[0] if both else None, None, 0)
        if k == 0 and levels > 1:
            rows_of = [value[2 * eighth : 2 * eighth + chunks] for value in held["four", 0]]
            group = functools.reduce(jnp.multiply, rows_of).reshape(1, channels)
            held["unit"] = group
            others = held["others"] = []
            for level in range(levels - 1):
                other = swap(group, 8 << level)
                others.append(other)
                group = group * other
        send(k)

    def parts(k):
        held["block", k], held["sofar"] = block_parts(k, held.get("sofar", ()))
        held["last"] = (held["block", k][6],)

    def taken(k, level):
        pay = held["level", k][0]
        return [lax.ppermute(pay, "seq", perm) for perm in level_perms(level)]

    def send(k):
        held["taken", k] = taken(k, held["level", k][3])

    def climb(k):
        _, both, enter, level = held["level", k]
        came = held["taken", k]
        operands = came + held["others"][:level] + ([enter] if level else [])
        pay, enter = small(
            functools.partial(level_kernel, span[k], level, len(came)),
            (flat_shape(k), pair_shape(k)), "level", *operands, both, held["unit"],
        )
        held["level", k] = (pay, both, enter, level + 1)
        held["last"] = (pay,)
        send(k)

    def top(k):
        _, _, enter, level = held["level", k]
        got = held["taken", k]
        operands = got + held["others"][:level] + ([enter] if level else [])
        mine, side, depth, corner = small(
            functools.partial(top_kernel, span[k], k, level, len(got)), (pair_shape(k),) * 4, "top",
            *operands, *held["four", k], *held["four", 0],
        )
        held["back", k] = (swap(corner, 6), swap(side, 2), swap(depth, 4), mine)
        held["last"] = (mine,)

    def device(k):
        kept, came = held["kept", k]
        made = pair_shape(k, 4)
        give, own = small(
            functools.partial(return_kernel, span[k]), (made, made), "return",
            *held["back", k], kept, came, decay, decay_other,
        )
        held["final", k] = (own, swap(give, 1))
        held["last"] = (give,)

    def end(k):
        own, took = held["final", k]
        blocks = [held["block", i] for i, (owner, _, _) in enumerate(tiles) if owner == k]
        out, din, dquery, dkey, *sums = finish(
            k, blocks, took, own, held["sofar"], held.get("prior", ())
        )
        held["prior"] = (*sums, dquery, dkey, out, din)
        held["last"] = (sums[0],)

    decay_other = swap(decay, 1)
    for k in every:
        sent, kept = device_states(k, (decay_other, held["last"][0]) if k else ())
        held["kept", k] = (kept, swap(sent, 1))
        held["last"] = (sent,)
    held["others"] = []

    steps = {
        "join": join, "parts": parts, "quad": quad, "climb": climb, "top": top,
        "device": device, "end": end,
    }
    for name, k in schedule(levels):
        steps[name](k)
    draw, dquery, dkey, out, din = held["prior"]
    return out, din, draw.T, dkey, dquery


def solution(mesh):
    sequence = P(("groups", "seq"), None)
    return jax.shard_map(
        local,
        mesh=mesh,
        in_specs=(
            sequence, sequence, sequence, sequence, P(), P(), P(("groups", "seq")), sequence,
        ),
        out_specs=(sequence,) * 5,
        check_vma=False,
    )
```

```python
import functools

import jax
import jax.numpy as jnp
from jax import lax
from jax.experimental import pallas as pl
from jax.experimental.pallas import tpu as pltpu
from jax.sharding import PartitionSpec as P

WIDTHS = (10, 10)
TILES = (5, 5)
SMALL_COST = 1000
STATES_COST = 4_000_000_000
VMEM_BYTES = 28 * 1024 * 1024

F32 = jnp.float32
BF16 = jnp.bfloat16


def dot_nn(left, right):
    return lax.dot_general(left, right, (((1,), (0,)), ((), ())), preferred_element_type=F32)


def dot_nt(left, right):
    return lax.dot_general(left, right, (((1,), (1,)), ((), ())), preferred_element_type=F32)


def halves(value):
    high = value.astype(BF16)
    return high, (value - high.astype(F32)).astype(BF16)


def sum_dot(matrix, value):
    first = value.astype(BF16)
    rest = value - first.astype(F32)
    second = rest.astype(BF16)
    third = (rest - second.astype(F32)).astype(BF16)
    return dot_nn(matrix, first) + dot_nn(matrix, second) + dot_nn(matrix, third)


def head_spread(depth, offset, head_count, first_column, columns, head_size):
    row = lax.broadcasted_iota(jnp.int32, (depth, columns), 0) - offset
    held = (row >= 0) & (row < 2 * head_count)
    row = jnp.where(row >= head_count, row - head_count, row)
    column = lax.broadcasted_iota(jnp.int32, (depth, columns), 1) + first_column
    inside = column - row * head_size
    return jnp.where(held & (inside >= 0) & (inside < head_size), 1.0, 0.0).astype(BF16)


def head_collect(head_count, first_column, columns, head_size):
    row = lax.broadcasted_iota(jnp.int32, (columns, head_count), 0) + first_column
    column = lax.broadcasted_iota(jnp.int32, (columns, head_count), 1)
    offset = row - column * head_size
    return jnp.where((offset >= 0) & (offset < head_size), 1.0, 0.0).astype(BF16)


def triangle(rows, lower):
    first = lax.broadcasted_iota(jnp.int32, (rows, rows), 0)
    second = lax.broadcasted_iota(jnp.int32, (rows, rows), 1)
    return (first >= second) if lower else (first <= second)


def start_counts(starts_row):
    rows = starts_row.shape[1]
    flags = starts_row.astype(F32)
    column = jnp.sum(jnp.where(triangle(rows, True), flags, 0.0), axis=1, keepdims=True)
    spread = jnp.broadcast_to(flags, (8, rows)).astype(BF16)
    row = dot_nn(spread, triangle(rows, False).astype(F32).astype(BF16))[:1]
    return column, row


def softplus(value):
    return jnp.maximum(value, 0.0) + jnp.log1p(jnp.exp(-jnp.abs(value)))


def sum_dot_left(value, matrix):
    first = value.astype(BF16)
    rest = value - first.astype(F32)
    second = rest.astype(BF16)
    third = (rest - second.astype(F32)).astype(BF16)
    return dot_nn(first, matrix) + dot_nn(second, matrix) + dot_nn(third, matrix)


def fetch(pairs, sems):
    copies = [
        pltpu.make_async_copy(source, target, sems.at[i])
        for i, (source, target) in enumerate(pairs)
    ]
    for copy in copies:
        copy.start()
    return copies


def prep_kernel(
    head_size, raw_hbm, rate_hbm, skip_hbm, starts_hbm, query_hbm, key_hbm,
    heads_ref, maps_ref, turned_ref, rows_ref, decay_ref,
    raw_ref, rate_ref, skip_ref, starts_ref, query_ref, key_ref, sems,
):
    copies = fetch(
        [
            (raw_hbm, raw_ref), (rate_hbm, rate_ref), (skip_hbm, skip_ref),
            (starts_hbm, starts_ref), (query_hbm, query_ref), (key_hbm, key_ref),
        ],
        sems,
    )
    head_count, rows = raw_ref.shape
    upper = triangle(rows, False).astype(F32).astype(BF16)
    for copy in copies:
        copy.wait()
    step = softplus(raw_ref[...])
    rate = jnp.broadcast_to(rate_ref[...], (8, head_count)).T[:, :1]
    cumulative = sum_dot_left(-step * rate, upper)
    count, _ = start_counts(starts_ref[...])
    in_lead = count == 0.0
    in_tail = count == count[rows - 1 :, :]
    state_size = query_ref.shape[1]
    lead = jnp.where(in_lead, query_ref[...].astype(F32), 0.0)
    tail = jnp.where(in_tail, key_ref[...].astype(F32), 0.0)
    maps_ref[:, :state_size] = lead.astype(BF16)
    maps_ref[:, state_size:] = tail.astype(BF16)
    turned_ref[:state_size] = lead.T.astype(BF16)
    turned_ref[state_size:] = tail.T.astype(BF16)
    fall = jnp.exp(cumulative).T
    grow = (jnp.exp(-cumulative) * step).T
    heads_ref[...] = jnp.concatenate(
        halves(fall)
        + halves(grow)
        + (
            jnp.where(in_lead, 1.0, 0.0).astype(BF16),
            jnp.where(in_tail, 1.0, 0.0).astype(BF16),
        ),
        axis=1,
    )
    channels = rows_ref.shape[1]
    spread = head_spread(2 * head_count, 0, head_count, 0, channels, head_size)

    def wide(value):
        return dot_nn(
            jnp.concatenate(halves(jnp.broadcast_to(value, (8, head_count))), axis=1), spread
        )[:1]

    last = wide(fall[rows - 1 :, :])
    decay = jnp.where(count[rows - 1 :, :] == 0.0, last, 0.0)
    rows_ref[0:1, :] = decay
    rows_ref[1:2, :] = last
    rows_ref[2:3, :] = wide(skip_ref[...])
    decay_ref[...] = decay


def place():
    index = lax.axis_index("seq")
    return ((index & 1) == 0, (index & 2) == 0, (index & 4) == 0), index >> 3


def outward(firsts, value):
    half = value.shape[0] // 2
    low, high = value[:half], value[half:]
    other, own = jnp.where(firsts[0], high, low), jnp.where(firsts[0], low, high)
    if len(firsts) > 1:
        other, own = outward(firsts[1:], other), outward(firsts[1:], own)
    return jnp.concatenate([other, own], axis=0)


def inward(firsts, other, own):
    if len(firsts) > 1:
        half = own.shape[0] // 2
        other = inward(firsts[1:], other[:half], other[half:])
        own = inward(firsts[1:], own[:half], own[half:])
    low, high = jnp.where(firsts[0], own, other), jnp.where(firsts[0], other, own)
    return jnp.concatenate([low, high], axis=0)


def joined(first, own_decay, other_decay, own, came):
    one = jnp.ones_like(own_decay)
    forward = (
        jnp.where(first, other_decay, one) * own[0] + jnp.where(first, one, own_decay) * came[0]
    )
    backward = (
        jnp.where(first, one, other_decay) * own[1] + jnp.where(first, own_decay, one) * came[1]
    )
    return forward, backward


def split_pair(first, own_decay, other_decay, own, came, entering, leaving, put_own, put_other):
    @pl.when(first)
    def _():
        put_own(0, entering)
        put_other(0, own_decay * entering + own(0))
        put_other(1, leaving)
        put_own(1, other_decay * leaving + came(1))

    @pl.when(jnp.logical_not(first))
    def _():
        put_other(0, entering)
        put_own(0, other_decay * entering + came(0))
        put_own(1, leaving)
        put_other(1, own_decay * leaving + own(1))


def join_kernel(columns, spans, kept_ref, came_ref, own_ref, other_ref, *results):
    firsts, _ = place()
    forward, backward = joined(
        firsts[0], own_ref[:, columns], other_ref[:, columns], kept_ref, came_ref
    )
    quarter = forward.shape[0] // 4
    for slot, ref in enumerate(results):
        here = slice(slot * quarter, (slot + 1) * quarter)
        ref[:quarter] = forward[here]
        ref[quarter : 2 * quarter] = backward[here]
        if ref.shape[0] > 2 * quarter:
            for chunk, there in enumerate(spans):
                row = 2 * quarter + chunk
                ref[row : row + 1, : there.stop - there.start] = (
                    own_ref[:, there] * other_ref[:, there]
                )


def four_chips(firsts, row, values, decays):
    half = decays[0].shape[0] - 8
    quarter = half // 2
    width = values[0].shape[1]
    return (
        in_order(firsts, *(ref[half + row : half + row + 1, :width] for ref in decays)),
        in_order(firsts, *(ref[:quarter] for ref in values)),
        in_order(firsts, *(ref[quarter:half] for ref in values)),
    )


def in_order(firsts, own, side, depth, corner):
    _, near, low = firsts
    first, second = jnp.where(near, own, side), jnp.where(near, side, own)
    third, fourth = jnp.where(near, depth, corner), jnp.where(near, corner, depth)
    return (
        jnp.where(low, first, third), jnp.where(low, second, fourth),
        jnp.where(low, third, first), jnp.where(low, fourth, second),
    )


def for_chips(firsts, values):
    _, near, low = firsts
    first, second = jnp.where(low, values[0], values[2]), jnp.where(low, values[1], values[3])
    third, fourth = jnp.where(low, values[2], values[0]), jnp.where(low, values[3], values[1])
    return (
        jnp.where(near, first, second), jnp.where(near, second, first),
        jnp.where(near, third, fourth), jnp.where(near, fourth, third),
    )


def quad_kernel(row, *refs):
    values, decays, results = refs[:4], refs[4:8], refs[8:]
    firsts, unit = place()
    decay, states, directs = four_chips(firsts, row, values, decays)
    forward, backward = states[0], directs[3]
    for i in (1, 2, 3):
        forward = decay[i] * forward + states[i]
        backward = directs[3 - i] + decay[3 - i] * backward
    results[0][...] = jnp.where((unit & 1) == 1, backward, forward)
    if len(results) > 1:
        results[1][0] = forward
        results[1][1] = backward


def absorb(columns, level, plane, taken_refs, others, enter_ref):
    upper = ((plane >> level) & 1) == 1
    taken = taken_refs[0][...]
    for ref in taken_refs[1:]:
        taken = taken + ref[...]
    if level == 0:
        zero = jnp.zeros_like(taken)
        return jnp.where(upper, taken, zero), jnp.where(upper, zero, taken)
    before = after = None
    for lower, ref in enumerate(others[:level]):
        other = ref[:, columns]
        above = ((plane >> lower) & 1) == 1
        one = jnp.ones_like(other)
        first = jnp.where(above, other, one)
        second = jnp.where(above, one, other)
        before = first if before is None else before * first
        after = second if after is None else after * second
    zero = jnp.zeros_like(before)
    return (
        enter_ref[0] + jnp.where(upper, before, zero) * taken,
        enter_ref[1] + jnp.where(upper, zero, after) * taken,
    )


def level_kernel(columns, level, taken_count, *refs):
    taken, refs = refs[:taken_count], refs[taken_count:]
    others, refs = refs[:level], refs[level:]
    enter_ref = None
    if level:
        enter_ref, refs = refs[0], refs[1:]
    both_ref, decay_ref, pay_ref, next_ref = refs
    _, plane = place()
    entering, leaving = absorb(columns, level, plane, taken, others, enter_ref)
    next_ref[0] = entering
    next_ref[1] = leaving
    upper = ((plane >> (level + 1)) & 1) == 1
    decay = decay_ref[:, columns]

    @pl.when(upper)
    def _():
        pay_ref[...] = decay * leaving + both_ref[1]

    @pl.when(jnp.logical_not(upper))
    def _():
        pay_ref[...] = decay * entering + both_ref[0]


def top_kernel(columns, row, level, taken_count, *refs):
    taken, refs = refs[:taken_count], refs[taken_count:]
    others, refs = refs[:level], refs[level:]
    enter_ref = None
    if level:
        enter_ref, refs = refs[0], refs[1:]
    values, decays, results = refs[:4], refs[4:8], refs[8:]
    firsts, unit = place()
    entering, leaving = absorb(columns, level, unit, taken, others, enter_ref)
    decay, states, directs = four_chips(firsts, row, values, decays)
    enters, leaves = [entering], [leaving]
    for i in (0, 1, 2):
        enters.append(decay[i] * enters[-1] + states[i])
        leaves.append(decay[3 - i] * leaves[-1] + directs[3 - i])
    for chain, value in enumerate((enters, leaves[::-1])):
        for ref, part in zip(results, for_chips(firsts, value)):
            ref[chain] = part


def return_kernel(columns, *refs):
    sources = refs[:4]
    kept_ref, came_ref, own_ref, other_ref, give_ref, stay_ref = refs[4:]
    first = place()[0][0]
    quarter = sources[0].shape[1]
    for slot, source in enumerate(sources):
        here = slice(slot * quarter, (slot + 1) * quarter)

        def put_own(chain, value, here=here):
            stay_ref[chain, here] = value

        def put_other(chain, value, here=here):
            give_ref[chain, here] = value

        split_pair(
            first, own_ref[:, columns], other_ref[:, columns],
            lambda i, here=here: kept_ref[i, here], lambda i, here=here: came_ref[i, here],
            source[0], source[1], put_own, put_other,
        )


def scale_columns(heads_ref, head_count, head_size, first, columns):
    heads = heads_ref[...]
    depth = heads.shape[1]
    args = (head_count, first, columns, head_size)
    fall = dot_nn(heads, head_spread(depth, 0, *args))
    grow = dot_nn(heads, head_spread(depth, 2 * head_count, *args))
    return fall, grow


def load_tiles(in_hbm, cot_hbm, in_ref, cot_ref, sems, first, tile):
    found = []
    for i in range(in_ref.shape[1] // tile):
        here = pl.ds(first + i * tile, tile)
        there = pl.ds(i * tile, tile)
        pair = []
        for j, (source, target) in enumerate(((in_hbm, in_ref), (cot_hbm, cot_ref))):
            copy = pltpu.make_async_copy(
                source.at[:, here], target.at[:, there], sems.at[2 * i + j]
            )
            copy.start()
            pair.append(copy)
        found.append(pair)
    return found


def states_kernel(
    head_count, head_size, first_column, tile, in_hbm, cot_hbm, heads_ref, turned_ref, rows_ref,
    send_ref, keep_ref, in_ref, cot_ref, sems,
):
    copies = load_tiles(in_hbm, cot_hbm, in_ref, cot_ref, sems, first_column, tile)
    firsts, _ = place()
    state_size = turned_ref.shape[0] // 2
    for i, pair in enumerate(copies):
        here = slice(i * tile, (i + 1) * tile)
        there = slice(first_column + i * tile, first_column + (i + 1) * tile)
        fall, grow = scale_columns(heads_ref, head_count, head_size, there.start, tile)
        for copy in pair:
            copy.wait()
        grown = (grow * in_ref[:, here].astype(F32)).astype(BF16)
        fallen = (fall * cot_ref[:, here].astype(F32)).astype(BF16)
        state = dot_nn(turned_ref[state_size:], grown) * rows_ref[1:2, there]
        direct = dot_nn(turned_ref[:state_size], fallen)
        half = state_size // 2
        for chain, value in enumerate((state, direct)):
            value = outward(firsts, value)
            send_ref[chain, :, here] = value[:half]
            keep_ref[chain, :, here] = value[half:]


def local_kernel(
    head_count, head_size, first_column, initial, final, in_hbm, cot_hbm, heads_ref, rows_ref,
    starts_ref, query_ref, key_ref, *refs,
):
    if not initial:
        score_ref, scoret_ref, total_in, refs = *refs[:3], refs[3:]
    out_ref, din_ref, grown_ref, fallen_ref, grow_ref, fall_ref, sums_ref = refs[:7]
    refs = refs[7:]
    if initial:
        (score_ref, scoret_ref), refs = refs[:2], refs[2:]
    (total_out, *key_out), (in_ref, cot_ref, sems) = refs[:-3], refs[-3:]
    rows, columns = in_ref.shape
    ((in_copy, cot_copy),) = load_tiles(
        in_hbm, cot_hbm, in_ref, cot_ref, sems, first_column, columns
    )
    if initial or final:
        column, row = start_counts(starts_ref[...])
        same = column == row
        allowed = same & triangle(rows, True)
    if initial:
        score_ref[...] = jnp.where(allowed, dot_nt(query_ref[...], key_ref[...]), 0.0).astype(BF16)
        scoret_ref[...] = jnp.where(
            same & triangle(rows, False), dot_nt(key_ref[...], query_ref[...]), 0.0
        ).astype(BF16)
    fall, grow = scale_columns(heads_ref, head_count, head_size, first_column, columns)
    fall_ref[...] = fall.astype(BF16)
    grow_ref[...] = grow.astype(BF16)
    collect = head_collect(head_count, first_column, columns, head_size)
    in_copy.wait()
    cot_copy.wait()
    in_wide = in_ref[...].astype(F32)
    cot_wide = cot_ref[...].astype(F32)
    skip = rows_ref[2:3, first_column : first_column + columns]
    grown = (grow * in_wide).astype(BF16)
    fallen = (fall * cot_wide).astype(BF16)
    grown_ref[...] = grown
    fallen_ref[...] = fallen
    total = dot_nt(fallen, grown)
    if not initial:
        total += total_in[...]
    produced = dot_nn(score_ref[...], grown)
    out_ref[...] = fall * produced + skip * in_wide
    sums_ref[0] = dot_nn((fallen.astype(F32) * produced).astype(BF16), collect)
    pulled = dot_nn(scoret_ref[...], fallen)
    din_ref[...] = grow * pulled + skip * cot_wide
    sums_ref[1] = dot_nn((grown.astype(F32) * pulled).astype(BF16), collect)
    if final:
        grads = jnp.where(allowed, total, 0.0)
        total_out[...] = dot_nn(grads.astype(BF16), key_ref[...])
        key_out[0][...] = dot_nn(grads.T.astype(BF16), query_ref[...])
    else:
        total_out[...] = total


def finish_kernel(
    head_count, head_size, first_column, tile, pieces, prior, final, *refs,
):
    blocks = [refs[7 * i : 7 * i + 7] for i in range(pieces)]
    (took_ref, own_ref, rows_ref, heads_ref, maps_ref) = refs[7 * pieces : 7 * pieces + 5]
    refs = refs[7 * pieces + 5 :]
    if final:
        (dquery_in, dkey_in, raw_ref, rate_ref), refs = refs[:4], refs[4:]
    if prior:
        (sums_in, edge_in, dlead_in, dtail_in), refs = refs[:4], refs[6:]
    out_hbm, din_hbm, dquery_ref, dkey_ref, *results, out_ref, din_ref, sems = refs
    state_size = maps_ref.shape[1] // 2
    rows = heads_ref.shape[0]
    firsts, _ = place()
    rise = sink = edge = dlead = dtail = None
    if prior:
        rise, sink, edge = sums_in[0], sums_in[1], edge_in[...]
        dlead, dtail = dlead_in[...], dtail_in[...]
    copies = []
    for i, block in enumerate(blocks):
        local_out_ref, local_din_ref, grown_ref, fallen_ref, grow_ref, fall_ref, sums_ref = block
        here = slice(i * tile, (i + 1) * tile)
        there = slice(first_column + i * tile, first_column + (i + 1) * tile)
        entering = inward(firsts, took_ref[0, :, here], own_ref[0, :, here])
        leaving = inward(firsts, took_ref[1, :, here], own_ref[1, :, here])
        grown = grown_ref[...]
        fallen = fallen_ref[...]
        entering_bf = entering.astype(BF16)
        leaving_bf = (leaving * rows_ref[1:2, there]).astype(BF16)
        reached = dot_nn(maps_ref[:, :state_size], entering_bf)
        behind = dot_nn(maps_ref[:, state_size:], leaving_bf)
        out_ref[:, here] = (local_out_ref[...] + fall_ref[...].astype(F32) * reached).astype(BF16)
        din_ref[:, here] = (local_din_ref[...] + grow_ref[...].astype(F32) * behind).astype(BF16)
        for j, (source, target) in enumerate(((out_ref, out_hbm), (din_ref, din_hbm))):
            copy = pltpu.make_async_copy(
                source.at[:, pl.ds(here.start, tile)], target.at[:, pl.ds(there.start, tile)],
                sems.at[2 * i + j],
            )
            copy.start()
            copies.append(copy)
        collect = head_collect(head_count, there.start, tile, head_size)
        rise_now = dot_nn((fallen.astype(F32) * reached).astype(BF16), collect) + sums_ref[0]
        pulled = grown.astype(F32) * behind
        sink_now = dot_nn(pulled.astype(BF16), collect) + sums_ref[1]
        edge_row = jnp.sum(pulled, axis=0, keepdims=True) + rows_ref[0:1, there] * jnp.sum(
            entering * leaving, axis=0, keepdims=True
        )
        high, rest = halves(jnp.broadcast_to(edge_row, (8, tile)))
        edge_now = dot_nn(high, collect) + dot_nn(rest, collect)
        dlead_now = dot_nt(fallen, entering_bf)
        dtail_now = dot_nt(grown, leaving_bf)
        rise = rise_now if rise is None else rise + rise_now
        sink = sink_now if sink is None else sink + sink_now
        edge = edge_now if edge is None else edge + edge_now
        dlead = dlead_now if dlead is None else dlead + dlead_now
        dtail = dtail_now if dtail is None else dtail + dtail_now
    if final:
        in_lead = heads_ref[:, 4 * head_count : 4 * head_count + 1].astype(F32) > 0.5
        in_tail = heads_ref[:, 4 * head_count + 1 : 4 * head_count + 2].astype(F32) > 0.5
        dquery_ref[...] = (dquery_in[...] + jnp.where(in_lead, dlead, 0.0)).astype(BF16)
        dkey_ref[...] = (dkey_in[...] + jnp.where(in_tail, dtail, 0.0)).astype(BF16)
        lower = triangle(rows, True).astype(F32).astype(BF16)
        sink_turned = sink.T
        later = sum_dot_left(rise.T - sink_turned, lower) + edge.T[:, :1]
        raw = raw_ref[...]
        rate = jnp.broadcast_to(rate_ref[...], (8, head_count)).T[:, :1]
        results[0][...] = (sink_turned / softplus(raw) - rate * later) / (1.0 + jnp.exp(-raw))
    else:
        dquery_ref[...] = dlead
        dkey_ref[...] = dtail
        results[0][0] = rise
        results[0][1] = sink
        results[1][...] = edge
    for copy in copies:
        copy.wait()


def schedule(levels):
    climbs = [("climb", k) for _ in range(levels - 1) for k in (0, 1)]
    middle = [("top", 0), ("quad", 1)]
    if climbs:
        middle = [("quad", 1), *climbs, ("top", 0)]
    return [
        ("join", 0), ("parts", 0), ("join", 1), ("parts", 1), ("quad", 0), ("parts", 2), *middle,
        ("parts", 3), ("top", 1), ("device", 0), ("end", 0), ("device", 1), ("end", 1),
    ]


def params():
    return pltpu.CompilerParams(vmem_limit_bytes=VMEM_BYTES)


def cost(flops, count):
    return pl.CostEstimate(flops=flops, bytes_accessed=count, transcendentals=0)


def after(kernel, count, extra):
    def run(*refs):
        kernel(*refs[:count], *refs[count + extra :])

    return run


ANY = pl.BlockSpec(memory_space=pl.ANY)
HBM = pl.BlockSpec(memory_space=pltpu.HBM)
NEAR = pl.BlockSpec(memory_space=pltpu.VMEM)


def local(inputs, raw_steps, input_map, output_map, decay_rates, skip_gain, starts, cotangent):
    rows, channels = inputs.shape
    head_count = decay_rates.shape[0]
    head_size = channels // head_count
    state_size = input_map.shape[1]
    eighth = state_size // 8
    unit = channels // sum(WIDTHS)
    widths = [count * unit for count in WIDTHS]
    tile_of = [count * unit for count in TILES]
    chunks = len(widths)
    firsts = [sum(widths[:k]) for k in range(chunks)]

    size = lax.axis_size("seq")
    planes = size // 8
    levels = planes.bit_length() - 1
    starts_row = starts.reshape(1, rows)
    rate_row = decay_rates.reshape(1, head_count)
    skip_heads = skip_gain.reshape(1, head_count)
    raw_turned = raw_steps.T

    def far(value):
        return pltpu.with_memory_space_constraint(value, pltpu.HBM)

    def shape(dims, kind=F32):
        return jax.ShapeDtypeStruct(dims, kind)

    heads, maps, turned, wide_rows, decay = pl.pallas_call(
        functools.partial(prep_kernel, head_size),
        out_shape=(
            shape((rows, 4 * head_count + 2), BF16),
            shape((rows, 2 * state_size), BF16),
            shape((2 * state_size, rows), BF16),
            shape((8, channels)),
            shape((1, channels)),
        ),
        in_specs=[HBM] * 6,
        scratch_shapes=[
            pltpu.VMEM((head_count, rows), F32), pltpu.VMEM((1, head_count), F32),
            pltpu.VMEM((1, head_count), F32), pltpu.VMEM((1, rows), jnp.int32),
            pltpu.VMEM((rows, state_size), BF16), pltpu.VMEM((rows, state_size), BF16),
            pltpu.SemaphoreType.DMA((6,)),
        ],
        compiler_params=params(),
        name="prep",
    )(*(far(v) for v in (raw_turned, rate_row, skip_heads, starts_row, output_map, input_map)))

    row_shape = shape((1, channels))

    def flat_shape(chunk):
        return shape((eighth, widths[chunk]))

    def pair_shape(chunk, scale=1):
        return shape((2, scale * eighth, widths[chunk]))

    def tile_scratch(chunk):
        block = (rows, widths[chunk])
        return [
            pltpu.VMEM(block, BF16), pltpu.VMEM(block, BF16),
            pltpu.SemaphoreType.DMA((2 * widths[chunk] // tile_of[chunk],)),
        ]

    def device_states(chunk, last):
        kernel = functools.partial(
            states_kernel, head_count, head_size, firsts[chunk], tile_of[chunk]
        )
        return pl.pallas_call(
            after(kernel, 5, len(last)),
            out_shape=(pair_shape(chunk, 4), pair_shape(chunk, 4)),
            in_specs=[HBM, HBM, NEAR, NEAR, NEAR] + [ANY] * len(last),
            scratch_shapes=tile_scratch(chunk),
            compiler_params=params(),
            cost_estimate=cost(STATES_COST, 1000),
            name="states",
        )(far(inputs), far(cotangent), heads, turned, wide_rows, *last)

    def swap(value, bit):
        return lax.ppermute(value, "seq", [(i, i ^ bit) for i in range(size)])

    def level_perms(level):
        span = 1 << level
        perms = []
        for shift in range(span):
            pairs = []
            for base in range(0, planes, 2 * span):
                pairs.append((base + span - 1, base + span + shift))
                pairs.append((base + span, base + span - 1 - shift))
            perms.append([(8 * a + r, 8 * b + r) for a, b in pairs for r in range(8)])
        return perms

    held = {"last": ()}

    def small(kernel, out_shape, name, *operands):
        last = held["last"]
        return pl.pallas_call(
            after(kernel, len(operands), len(last)),
            out_shape=out_shape,
            in_specs=[NEAR] * len(operands) + [ANY] * len(last),
            compiler_params=params(),
            cost_estimate=cost(SMALL_COST, 1000),
            name=name,
        )(*operands, *last)

    tiles = [
        (k, firsts[k] + i * tile_of[k], tile_of[k])
        for k in range(chunks)
        for i in range(widths[k] // tile_of[k])
    ]

    def block_parts(piece, sofar):
        last = held["last"]
        initial = piece == 0
        final = piece == len(tiles) - 1
        _, first, tile = tiles[piece]
        square = (rows, rows)
        block = (rows, tile)
        outs = [shape(block)] * 2 + [shape(block, BF16)] * 4 + [shape((2, rows, head_count))]
        if initial:
            outs += [shape(square, BF16), shape(square, BF16)]
        outs += [shape((rows, state_size))] * 2 if final else [shape(square)]
        operands = [
            far(inputs), far(cotangent), heads, wide_rows, starts_row, output_map, input_map,
        ] + list(sofar)
        kernel = functools.partial(local_kernel, head_count, head_size, first, initial, final)
        made = pl.pallas_call(
            after(kernel, len(operands), len(last)),
            out_shape=tuple(outs),
            in_specs=[HBM, HBM] + [NEAR] * (len(operands) - 2) + [ANY] * len(last),
            scratch_shapes=[
                pltpu.VMEM(block, BF16), pltpu.VMEM(block, BF16), pltpu.SemaphoreType.DMA((2,)),
            ],
            compiler_params=params(),
            cost_estimate=cost(1000, 1000),
            name="block",
        )(*operands, *last)
        if final:
            return made[:7], tuple(made[-2:])
        if initial:
            return made[:7], tuple(made[7:])
        return made[:7], (sofar[0], sofar[1], made[7])

    def finish(chunk, blocks, took, own, grads, prior):
        flat = (rows, state_size)
        tile = tile_of[chunk]
        last = held["last"]
        final = chunk == chunks - 1
        operands = [value for block in blocks for value in block]
        operands += [took, own, wide_rows, heads, maps]
        if final:
            operands += [*grads, raw_turned, rate_row]
        in_specs = [NEAR] * len(operands)
        aliases = {}
        if prior:
            aliases = {len(operands) + 4: 0, len(operands) + 5: 1}
            operands += list(prior)
            in_specs += [NEAR] * 4 + [ANY, ANY]
        kind = BF16 if final else F32
        ends = [shape((head_count, rows))]
        if not final:
            ends = [shape((2, rows, head_count)), shape((8, head_count))]
        kernel = functools.partial(
            finish_kernel, head_count, head_size, firsts[chunk], tile, len(blocks), bool(prior),
            final,
        )
        result = shape((rows, widths[chunk]), BF16)
        return pl.pallas_call(
            after(kernel, len(operands), len(last)),
            out_shape=(
                shape((rows, channels), BF16), shape((rows, channels), BF16),
                shape(flat, kind), shape(flat, kind), *ends,
            ),
            in_specs=in_specs + [ANY] * len(last),
            out_specs=(ANY, ANY, NEAR, NEAR) + (NEAR,) * len(ends),
            scratch_shapes=[
                pltpu.VMEM(result.shape, BF16), pltpu.VMEM(result.shape, BF16),
                pltpu.SemaphoreType.DMA((2 * widths[chunk] // tile,)),
            ],
            input_output_aliases=aliases,
            compiler_params=params(),
            cost_estimate=cost(1000, 1000),
            name="finish",
        )(*operands, *last)

    every = range(chunks)
    span = [slice(firsts[k], firsts[k] + widths[k]) for k in every]

    def join(k):
        kept, came = held["kept", k]
        part = shape((2 * eighth + (8 if k == 0 else 0), widths[k]))
        corner, side, depth, stay = small(
            functools.partial(join_kernel, span[k], span), (part,) * 4, "join",
            kept, came, decay, decay_other,
        )
        held["last"] = (side,)
        held["four", k] = (stay, swap(side, 2), swap(depth, 4), swap(corner, 6))

    def quad(k):
        made = (flat_shape(k),) + ((pair_shape(k),) if levels > 1 else ())
        pay, *both = small(
            functools.partial(quad_kernel, k), made, "quad", *held["four", k], *held["four", 0],
        )
        held["last"] = (pay,)
        held["level", k] = (pay, both[0] if both else None, None, 0)
        if k == 0 and levels > 1:
            product = functools.reduce(jnp.multiply, held["four", 0])[2 * eighth :]
            group = jnp.concatenate(
                [product[i : i + 1, : widths[i]] for i in every], axis=1
            )
            held["unit"] = group
            others = held["others"] = []
            for level in range(levels - 1):
                other = swap(group, 8 << level)
                others.append(other)
                group = group * other
        send(k)

    def parts(k):
        held["block", k], held["sofar"] = block_parts(k, held.get("sofar", ()))
        held["last"] = (held["block", k][6],)

    def taken(k, level):
        pay = held["level", k][0]
        return [lax.ppermute(pay, "seq", perm) for perm in level_perms(level)]

    def send(k):
        held["taken", k] = taken(k, held["level", k][3])

    def climb(k):
        _, both, enter, level = held["level", k]
        came = held["taken", k]
        operands = came + held["others"][:level] + ([enter] if level else [])
        pay, enter = small(
            functools.partial(level_kernel, span[k], level, len(came)),
            (flat_shape(k), pair_shape(k)), "level", *operands, both, held["unit"],
        )
        held["level", k] = (pay, both, enter, level + 1)
        held["last"] = (pay,)
        send(k)

    def top(k):
        _, _, enter, level = held["level", k]
        got = held["taken", k]
        operands = got + held["others"][:level] + ([enter] if level else [])
        mine, side, depth, corner = small(
            functools.partial(top_kernel, span[k], k, level, len(got)), (pair_shape(k),) * 4, "top",
            *operands, *held["four", k], *held["four", 0],
        )
        held["back", k] = (swap(corner, 6), swap(side, 2), swap(depth, 4), mine)
        held["last"] = (mine,)

    def device(k):
        kept, came = held["kept", k]
        made = pair_shape(k, 4)
        give, own = small(
            functools.partial(return_kernel, span[k]), (made, made), "return",
            *held["back", k], kept, came, decay, decay_other,
        )
        held["final", k] = (own, swap(give, 1))
        held["last"] = (give,)

    def end(k):
        own, took = held["final", k]
        blocks = [held["block", i] for i, (owner, _, _) in enumerate(tiles) if owner == k]
        out, din, dquery, dkey, *sums = finish(
            k, blocks, took, own, held["sofar"], held.get("prior", ())
        )
        held["prior"] = (*sums, dquery, dkey, out, din)
        held["last"] = (sums[0],)

    decay_other = swap(decay, 1)
    for k in every:
        sent, kept = device_states(k, (decay_other, held["last"][0]) if k else ())
        held["kept", k] = (kept, swap(sent, 1))
        held["last"] = (sent,)
    held["others"] = []

    steps = {
        "join": join, "parts": parts, "quad": quad, "climb": climb, "top": top,
        "device": device, "end": end,
    }
    for name, k in schedule(levels):
        steps[name](k)
    draw, dquery, dkey, out, din = held["prior"]
    return out, din, draw.T, dkey, dquery


def solution(mesh):
    sequence = P(("groups", "seq"), None)
    return jax.shard_map(
        local,
        mesh=mesh,
        in_specs=(
            sequence, sequence, sequence, sequence, P(), P(), P(("groups", "seq")), sequence,
        ),
        out_specs=(sequence,) * 5,
        check_vma=False,
    )
```
